256 devices in a mesh: tok: 4 (over z_lo), row: 8 (over y, z_hi), col: 8 (over x, core).
Axes of the slice: x: 4, y: 4, z: 8 (z_hi: 2, z_lo: 4; z = z_hi * 4 + z_lo), core: 2. Of those that a mesh axis runs over, the one named last changes fastest.
Arguments:
- tokens: bfloat16 [1024, 8192], P('tok', 'row'), may hold values from -6 to 6
- cotangent: bfloat16 [1024, 8192], P('tok', 'row'), may hold values from -6 to 6
- gate_weight: bfloat16 [8192, 16384], P('row', ('tok', 'col')), may hold values from -0.0625 to 0.0625
- up_weight: bfloat16 [8192, 16384], P('row', ('tok', 'col')), may hold values from -0.0625 to 0.0625
- down_weight: bfloat16 [16384, 8192], P(('tok', 'col'), 'row'), may hold values from -0.046875 to 0.046875
- gate_keep: int32 [512, 16384], P('row', ('tok', 'col')), may hold values from 0 to 65535
- up_keep: int32 [512, 16384], P('row', ('tok', 'col')), may hold values from 0 to 65535
- down_keep: int32 [1024, 8192], P(('tok', 'col'), 'row'), may hold values from 0 to 65535
Outputs:
- input_grad: bfloat16 [1024, 8192], P('tok', 'row')
- gate_grad: bfloat16 [8192, 16384], P('row', ('tok', 'col'))
- up_grad: bfloat16 [8192, 16384], P('row', ('tok', 'col'))
- down_grad: bfloat16 [16384, 8192], P(('tok', 'col'), 'row')
- gate_score: bfloat16 [8192, 16384], P('row', ('tok', 'col'))
- up_score: bfloat16 [8192, 16384], P('row', ('tok', 'col'))
- down_score: bfloat16 [16384, 8192], P(('tok', 'col'), 'row')
The draws below stay inside these ranges and needn't reach their ends.
All inputs are finite; a program needn't handle non-finite values.
Results may differ from the reference program's by a relative error of at most 0.005.
Values may be sent and summed in bfloat16 or wider, within the bound.
A program may use at most 128 MiB of HBM per device.

```python
import jax
import jax.numpy as jnp

D = 8192
F = 16384
TOKENS = 1024
N_ROW = 8


def place_ends(drawn, own_key, low, top_value):
    spot = [jax.random.randint(jax.random.fold_in(own_key, axis), (), 0, length) for axis, length in enumerate(drawn.shape)]
    main_axis = drawn.shape.index(max(drawn.shape))
    next_to = spot[:main_axis] + [(spot[main_axis] + 1) % drawn.shape[main_axis]] + spot[main_axis + 1:]
    return drawn.at[tuple(spot)].set(low).at[tuple(next_to)].set(top_value)


def level_of(key, dims, pieces, least, top_value):
    def one(position, blocks):
        steps = jax.random.uniform(jax.random.fold_in(jax.random.fold_in(key, 6), position), (blocks,), jnp.float32, least / len(pieces), top_value / len(pieces))
        return jnp.repeat(jnp.exp(steps), dims[position] // blocks).reshape((-1,) + (1,) * (len(dims) - position - 1))

    factor_of = one(*pieces[0])
    for cut in pieces[1:]:
        factor_of = factor_of * one(*cut)
    return factor_of


def normal_values(stream_key, extent, deviation, bound, pieces=(), kind=jnp.bfloat16):
    result = deviation * jax.random.normal(stream_key, extent, jnp.float32)
    if pieces:
        result = result * level_of(stream_key, extent, pieces, -0.22, 0.18)
    return jnp.clip(result, -bound, bound).astype(kind)


def setup_inputs(seed: int = 0) -> dict:
    arg_keys = jax.random.split(jax.random.key(seed), 9)
    tokens = normal_values(arg_keys[0], (TOKENS, D), 1.0, 6.0, ((0, 4), (1, 8)))
    cotangent = normal_values(arg_keys[1], (TOKENS, D), 1.0, 6.0, ((0, 4), (1, 8)))
    gate_weight = normal_values(arg_keys[2], (D, F), D ** -0.5, 0.0625, ((0, 8), (1, 32)))
    up_weight = normal_values(arg_keys[3], (D, F), D ** -0.5, 0.0625, ((0, 8), (1, 32)))
    down_weight = normal_values(arg_keys[4], (F, D), F ** -0.5, 0.046875, ((0, 32), (1, 8)))
    gate_keep = place_ends(jax.random.randint(arg_keys[5], (D // 16, F), 0, 65536), jax.random.fold_in(arg_keys[5], 1), 0, 65535).astype(jnp.int32)
    up_keep = place_ends(jax.random.randint(arg_keys[6], (D // 16, F), 0, 65536), jax.random.fold_in(arg_keys[6], 1), 0, 65535).astype(jnp.int32)
    down_keep = place_ends(jax.random.randint(arg_keys[7], (F // 16, D), 0, 65536), jax.random.fold_in(arg_keys[7], 1), 0, 65535).astype(jnp.int32)
    return dict(tokens=tokens, cotangent=cotangent, gate_weight=gate_weight, up_weight=up_weight, down_weight=down_weight, gate_keep=gate_keep, up_keep=up_keep, down_keep=down_keep)


def unpack_bits(packed):
    shifts = jnp.arange(16, dtype=jnp.int32)
    flags = jnp.right_shift(packed[:, None, :], shifts[None, :, None]) & 1
    return flags.reshape(packed.shape[0] * 16, packed.shape[1])


def reference(tokens, cotangent, gate_weight, up_weight, down_weight, gate_keep, up_keep, down_keep):
    gate_mask = unpack_bits(gate_keep).astype(jnp.bfloat16)
    up_mask = unpack_bits(up_keep).astype(jnp.bfloat16)
    down_mask = unpack_bits(down_keep).astype(jnp.bfloat16)
    gate_eff = gate_weight * gate_mask
    up_eff = up_weight * up_mask
    down_eff = down_weight * down_mask
    block_width = D // N_ROW
    gate_pre = jnp.zeros((TOKENS, F), jnp.float32)
    up_pre = jnp.zeros((TOKENS, F), jnp.float32)
    back_pre = jnp.zeros((TOKENS, F), jnp.float32)
    for block_idx in range(N_ROW):
        lower = block_idx * block_width
        upper = lower + block_width
        gate_pre = gate_pre + jnp.dot(tokens[:, lower:upper], gate_eff[lower:upper, :], preferred_element_type=jnp.float32)
        up_pre = up_pre + jnp.dot(tokens[:, lower:upper], up_eff[lower:upper, :], preferred_element_type=jnp.float32)
        back_pre = back_pre + jnp.dot(cotangent[:, lower:upper], down_eff[:, lower:upper].T, preferred_element_type=jnp.float32)
    sigmoid_val = jax.nn.sigmoid(gate_pre)
    silu_value = gate_pre * sigmoid_val
    hidden = (silu_value * up_pre).astype(jnp.bfloat16)
    derivative = sigmoid_val * (1.0 + gate_pre * (1.0 - sigmoid_val))
    gate_back = (back_pre * up_pre * derivative).astype(jnp.bfloat16)
    up_back = (back_pre * silu_value).astype(jnp.bfloat16)
    down_full = jnp.dot(hidden.T, cotangent, preferred_element_type=jnp.float32)
    gate_full = jnp.dot(tokens.T, gate_back, preferred_element_type=jnp.float32)
    up_full = jnp.dot(tokens.T, up_back, preferred_element_type=jnp.float32)
    gate_grad = (gate_full * gate_mask.astype(jnp.float32)).astype(jnp.bfloat16)
    up_grad = (up_full * up_mask.astype(jnp.float32)).astype(jnp.bfloat16)
    down_grad = (down_full * down_mask.astype(jnp.float32)).astype(jnp.bfloat16)
    gate_score = (-(gate_weight.astype(jnp.float32) * gate_full)).astype(jnp.bfloat16)
    up_score = (-(up_weight.astype(jnp.float32) * up_full)).astype(jnp.bfloat16)
    down_score = (-(down_weight.astype(jnp.float32) * down_full)).astype(jnp.bfloat16)
    input_full = jnp.dot(gate_back, gate_eff.T, preferred_element_type=jnp.float32) + jnp.dot(up_back, up_eff.T, preferred_element_type=jnp.float32)
    input_grad = input_full.astype(jnp.bfloat16)
    return input_grad, gate_grad, up_grad, down_grad, gate_score, up_score, down_score
```

```python
import functools

import jax
import jax.numpy as jnp
from jax import lax
from jax.experimental import pallas as pl
from jax.experimental.pallas import tpu as pltpu
from jax.sharding import PartitionSpec as P

MESH = pl.DeviceIdType.MESH
BF = jnp.bfloat16
F32 = jnp.float32
NCH = 8
T = 128
H = 16
LAG = dict(ax=-2, ac=-1, s1=0, s2=0, s3=1, s4=2, s5=3, s6=4, s7=5, s8=6)
ORDER = ("ax", "ac", "s1", "s2", "s3", "s4", "s5", "s6", "s7", "s8")


def apply_mask(w_ref, keep_ref):
    cols = w_ref.shape[1]
    shifts = lax.broadcasted_iota(jnp.int32, (16, cols), 0)

    def one(i, _):
        row = jnp.broadcast_to(keep_ref[pl.ds(i, 1), :], (16, cols))
        bits = (jnp.right_shift(row, shifts) & 1).astype(F32)
        at = pl.ds(pl.multiple_of(i * 16, 16), 16)
        w_ref[at, :] = (w_ref[at, :].astype(F32) * bits).astype(BF)
        return 0

    lax.fori_loop(0, keep_ref.shape[0], one, 0, unroll=4)


def comm_kernel(
    tokens, cot, gate_w, up_w, down_w, gate_k, up_k, down_k,
    out, tc_out, g_out,
    tc, gw, uw, dw, gk, uk, dk, pre, pre32, rx1, acc, rx3, hs, hr, keep, act,
    dpart, d32, dr, zown, zs, zr, obuf,
    ld_sem, send_sem, az, ax, ac, s1, s3, hrs, gh, gy, drs, zrs, ors, st_sem,
):
    t = lax.axis_index("tok")
    r = lax.axis_index("row")
    c = lax.axis_index("col")
    y, h = r // 2, r % 2
    x, k = c // 2, c % 2
    y_next, y_prev, y_opp = (y + 1) % 4, (y + 3) % 4, (y + 2) % 4
    at_next, at_prev = (t, y_next * 2 + h, c), (t, y_prev * 2 + h, c)
    at_twin = (t, y * 2 + (1 - h), c)
    at_core = (t, r, x * 2 + (1 - k))

    def tok_xor(n):
        return (t % 2 + n % 2) % 2 + 2 * ((t // 2 + n // 2) % 2)

    mine = pl.ds(pl.multiple_of(t * 256, 256), 256)
    loads = [
        pltpu.make_async_copy(src, dst, ld_sem.at[n])
        for n, (src, dst) in enumerate(
            (
                (tokens, tc.at[0, mine]), (cot, tc.at[1, mine]),
                (gate_k, gk), (gate_w, gw), (up_k, uk), (up_w, uw),
                (down_k, dk), (down_w, dw),
            )
        )
    ]
    for copy in loads:
        copy.start()

    barrier = pltpu.get_barrier_semaphore()
    peers = [at_next, at_prev, at_twin]
    peers += [(t, r, (c + n) % 8) for n in range(1, 8)]
    peers += [(tok_xor(n), r, c) for n in range(1, 4)]
    for peer in peers:
        pl.semaphore_signal(barrier, inc=1, device_id=peer, device_id_type=MESH)

    SEND = dict(az=0, ax=1, ac=2, rs=3, ag=4, d=5, z=6, o=7)

    def send(src, dst, cls, recv, peer):
        pltpu.make_async_remote_copy(
            src_ref=src, dst_ref=dst, send_sem=send_sem.at[SEND[cls]], recv_sem=recv,
            device_id=peer, device_id_type=MESH,
        ).start()

    def wait(ref, sem):
        pltpu.make_async_copy(ref, ref, sem).wait()

    def base(i):
        return tok_xor(i // 2) * 256 + (i % 2) * T

    def rows(i, q, n=H):
        return pl.ds(pl.multiple_of(base(i) + q * n, n), n)

    def stage_az(i):
        at = pl.ds(pl.multiple_of(t * 256 + (i % 2) * T + x * 32, 32), 32)
        send(tc.at[k, at], tc.at[k, at], "az", az.at[i], (tok_xor(i // 2), r, c))

    def stage_ax(i):
        if i < 2:
            return
        at = rows(i, x, 32)
        wait(tc.at[k, at], az.at[i])
        for n in (1, 3, 2):
            send(tc.at[k, at], tc.at[k, at], "ax", ax.at[i], (t, r, ((x + n) % 4) * 2 + k))

    def stage_ac(i):
        if i < 2:
            return
        wait(tc.at[k, pl.ds(0, 96)], ax.at[i])
        at = rows(i, 0, T)
        send(tc.at[k, at], tc.at[k, at], "ac", ac.at[i], at_core)

    def stage_s1(i):
        at = rows(i, 0, T)
        if i >= 2:
            wait(tc.at[1 - k, at], ac.at[i])
        tok_rows = tc[0, at, :]
        cot_rows = tc[1, at, :]
        parts = (
            jnp.dot(tok_rows, gw[...], preferred_element_type=F32),
            jnp.dot(tok_rows, uw[...], preferred_element_type=F32),
            lax.dot_general(
                cot_rows, dw[...], (((1,), (1,)), ((), ())), preferred_element_type=F32
            ),
        )
        for n, part in enumerate(parts):
            pre32[at, pl.ds(n * 512, 512)] = part
            pre[at, pl.ds(n * 512, 512)] = part.astype(BF)
        send(pre.at[rows(i, y_opp * 2)], rx1.at[i, 0], "rs", s1.at[i], at_next)
        send(pre.at[rows(i, y_opp * 2 + 1)], rx1.at[i, 1], "rs", s1.at[i], at_prev)
        send(pre.at[rows(i, y_next * 2 + 1)], rx3.at[i, 0], "rs", s3.at[i], at_next)
        send(pre.at[rows(i, y_prev * 2)], rx3.at[i, 1], "rs", s3.at[i], at_prev)

    def stage_s2(i):
        wait(rx1.at[i], s1.at[i])
        acc[i, 0] = (rx1[i, 0].astype(F32) + pre32[rows(i, y_next * 2), :]).astype(BF)
        send(acc.at[i, 0], rx3.at[i, 2], "rs", s3.at[i], at_next)
        acc[i, 1] = (rx1[i, 1].astype(F32) + pre32[rows(i, y_prev * 2 + 1), :]).astype(BF)
        send(acc.at[i, 1], rx3.at[i, 3], "rs", s3.at[i], at_prev)

    def stage_s3(i):
        wait(rx3.at[i], s3.at[i])

        def total(half):
            return (
                pre32[rows(i, y * 2 + half), :]
                + rx3[i, 1 - half].astype(F32)
                + rx3[i, 2 + half].astype(F32)
            )

        hs[i] = total(1 - h).astype(BF)
        send(hs.at[i], hr.at[i], "rs", hrs.at[i], at_twin)
        keep[i] = total(h)

    def stage_s4(i):
        wait(hr.at[i], hrs.at[i])
        sums = keep[i] + hr[i].astype(F32)
        gate, up, back = sums[:, :512], sums[:, 512:1024], sums[:, 1024:]
        sig = jax.nn.sigmoid(gate)
        silu = gate * sig
        at = rows(i, r)
        act[at, pl.ds(0, 512)] = (silu * up).astype(BF)
        act[at, pl.ds(512, 512)] = (back * up * (sig * (1.0 + gate * (1.0 - sig)))).astype(BF)
        act[at, pl.ds(1024, 512)] = (back * silu).astype(BF)
        send(act.at[at], act.at[at], "ag", gh.at[i], at_twin)
        send(act.at[at], act.at[at], "ag", gy.at[i, h], at_next)
        send(act.at[at], act.at[at], "ag", gy.at[i, 1 - h], at_prev)

    def stage_s5(i):
        at = rows(i, y * 2 + (1 - h))
        wait(act.at[at], gh.at[i])
        send(act.at[at], act.at[at], "ag", gy.at[i, 1 - h], at_next)
        send(act.at[at], act.at[at], "ag", gy.at[i, h], at_prev)

    def stage_s6(i):
        wait(act.at[pl.ds(0, 2 * H)], gy.at[i, 0])
        at = rows(i, y_prev * 2)
        send(act.at[at], act.at[at], "ag", gy.at[i, 1], at_next)
        at = rows(i, y_next * 2 + 1)
        send(act.at[at], act.at[at], "ag", gy.at[i, 1], at_prev)

    def stage_s7(i):
        wait(act.at[pl.ds(0, 4 * H)], gy.at[i, 1])
        at = rows(i, 0, T)
        nt = (((1,), (1,)), ((), ()))
        part = lax.dot_general(
            act[at, pl.ds(512, 512)], gw[...], nt, preferred_element_type=F32
        ) + lax.dot_general(
            act[at, pl.ds(1024, 512)], uw[...], nt, preferred_element_type=F32
        )
        d32[i] = part
        dpart[at, :] = part.astype(BF)
        for n in range(7):
            peer = (c + n + 1) % 8
            send(dpart.at[rows(i, peer)], dr.at[i, n], "d", drs.at[i], (t, r, peer))

    def stage_s8(i):
        wait(dr.at[i], drs.at[i])
        total = d32[i, pl.ds(pl.multiple_of(c * H, H), H), :]
        for n in range(7):
            total = total + dr[i, n].astype(F32)
        if i < 2:
            zown[i] = total
        else:
            zs[i - 2] = total
            send(zs.at[i - 2], zr.at[i - 2], "z", zrs.at[i - 2], (tok_xor(i // 2), r, c))

    def stage_s9(u):
        total = zown[u]
        for n in range(3):
            wait(zr.at[2 * n + u], zrs.at[2 * n + u])
            total = total + zr[2 * n + u]
        at = pl.ds(pl.multiple_of(u * T + c * H, H), H)
        obuf[at, :] = total.astype(BF)
        for n in range(7):
            send(obuf.at[at], obuf.at[at], "o", ors.at[u], (t, r, (c + n + 1) % 8))

    loads[0].wait()
    loads[1].wait()
    pl.semaphore_wait(barrier, len(peers))
    for i in range(2, NCH):
        stage_az(i)
    for n, (w, kk) in enumerate(((gw, gk), (uw, uk), (dw, dk))):
        loads[2 + 2 * n].wait()
        loads[3 + 2 * n].wait()
        apply_mask(w, kk)

    stages = dict(
        ax=stage_ax, ac=stage_ac, s1=stage_s1, s2=stage_s2, s3=stage_s3, s4=stage_s4,
        s5=stage_s5, s6=stage_s6, s7=stage_s7, s8=stage_s8,
    )
    for tick in range(min(LAG.values()), NCH + max(LAG.values())):
        for name in ORDER:
            i = tick - LAG[name]
            if 0 <= i < NCH:
                stages[name](i)
                if name == "s7" and i == NCH - 1:
                    stores = [
                        pltpu.make_async_copy(tc, tc_out, st_sem.at[0]),
                        pltpu.make_async_copy(act, g_out, st_sem.at[1]),
                    ]
                    for copy in stores:
                        copy.start()
                if name == "s8" and i >= NCH - 2:
                    stage_s9(i - (NCH - 2))
    for u in range(2):
        wait(obuf.at[pl.ds(0, 7 * H)], ors.at[u])
    last = pltpu.make_async_copy(obuf, out, st_sem.at[2])
    last.start()
    for copy in stores + [last]:
        copy.wait()
    wait(tc.at[0, pl.ds(0, 6 * 32)], send_sem.at[0])
    wait(tc.at[0, pl.ds(0, 18 * 32)], send_sem.at[1])
    wait(tc.at[0, pl.ds(0, 6 * T)], send_sem.at[2])
    wait(pre.at[pl.ds(0, 56 * H)], send_sem.at[3])
    wait(act.at[pl.ds(0, 56 * H)], send_sem.at[4])
    wait(dpart.at[pl.ds(0, 56 * H)], send_sem.at[5])
    wait(zs, send_sem.at[6])
    wait(obuf.at[pl.ds(0, 14 * H)], send_sem.at[7])


def grad_kernel(
    tok, cot, hidden, gate_back, up_back, gate_w, up_w, down_w, gate_k, up_k, down_k,
    gate_g, up_g, down_g, gate_s, up_s, down_s,
):
    def finish(full, w_ref, keep_ref, g_ref, s_ref):
        n, cols = keep_ref.shape
        shifts = lax.broadcasted_iota(jnp.int32, (16, cols), 0)
        s_ref[...] = (-(w_ref[...].astype(F32) * full)).astype(BF)
        for i in range(n):
            row = jnp.broadcast_to(keep_ref[i : i + 1, :], (16, cols))
            bits = (jnp.right_shift(row, shifts) & 1).astype(F32)
            g_ref[16 * i : 16 * i + 16, :] = (full[16 * i : 16 * i + 16, :] * bits).astype(BF)

    tn = (((0,), (0,)), ((), ()))
    left = tok[0]
    full = lax.dot_general(left, gate_back[...], tn, preferred_element_type=F32)
    finish(full, gate_w, gate_k, gate_g, gate_s)
    full = lax.dot_general(left, up_back[...], tn, preferred_element_type=F32)
    finish(full, up_w, up_k, up_g, up_s)
    full = lax.dot_general(hidden[...], cot[0], tn, preferred_element_type=F32)
    finish(full, down_w, down_k, down_g, down_s)


def on_device(tokens, cot, gate_w, up_w, down_w, gate_k, up_k, down_k):
    any_spec = pl.BlockSpec(memory_space=pltpu.HBM)
    dma = pltpu.SemaphoreType.DMA
    out, tc, act = pl.pallas_call(
        comm_kernel,
        name="exchange",
        out_shape=(
            jax.ShapeDtypeStruct((256, 1024), BF),
            jax.ShapeDtypeStruct((2, 1024, 1024), BF),
            jax.ShapeDtypeStruct((1024, 1536), BF),
        ),
        in_specs=[any_spec] * 8,
        out_specs=(any_spec,) * 3,
        scratch_shapes=[
            pltpu.VMEM((2, 1024, 1024), BF),
            pltpu.VMEM((1024, 512), BF),
            pltpu.VMEM((1024, 512), BF),
            pltpu.VMEM((512, 1024), BF),
            pltpu.VMEM((64, 512), jnp.int32),
            pltpu.VMEM((64, 512), jnp.int32),
            pltpu.VMEM((32, 1024), jnp.int32),
            pltpu.VMEM((1024, 1536), BF),
            pltpu.VMEM((1024, 1536), F32),
            pltpu.VMEM((NCH, 2, H, 1536), BF),
            pltpu.VMEM((NCH, 2, H, 1536), BF),
            pltpu.VMEM((NCH, 4, H, 1536), BF),
            pltpu.VMEM((NCH, H, 1536), BF),
            pltpu.VMEM((NCH, H, 1536), BF),
            pltpu.VMEM((NCH, H, 1536), F32),
            pltpu.VMEM((1024, 1536), BF),
            pltpu.VMEM((1024, 1024), BF),
            pltpu.VMEM((NCH, T, 1024), F32),
            pltpu.VMEM((NCH, 7, H, 1024), BF),
            pltpu.VMEM((2, H, 1024), F32),
            pltpu.VMEM((6, H, 1024), F32),
            pltpu.VMEM((6, H, 1024), F32),
            pltpu.VMEM((256, 1024), BF),
            dma((8,)),
            dma((8,)),
            dma((NCH,)),
            dma((NCH,)),
            dma((NCH,)),
            dma((NCH,)),
            dma((NCH,)),
            dma((NCH,)),
            dma((NCH,)),
            dma((NCH, 2)),
            dma((NCH,)),
            dma((6,)),
            dma((2,)),
            dma((3,)),
        ],
        compiler_params=pltpu.CompilerParams(
            collective_id=0, has_side_effects=True, vmem_limit_bytes=48 * 2**20
        ),
    )(tokens, cot, gate_w, up_w, down_w, gate_k, up_k, down_k)

    n = 4
    wide = pl.BlockSpec((1024 // n, 512), lambda i: (i, 0))
    tall = pl.BlockSpec((512 // n, 1024), lambda i: (i, 0))
    wide_keep = pl.BlockSpec((64 // n, 512), lambda i: (i, 0))
    tall_keep = pl.BlockSpec((32 // n, 1024), lambda i: (i, 0))
    up_shape = jax.ShapeDtypeStruct((1024, 512), BF)
    down_shape = jax.ShapeDtypeStruct((512, 1024), BF)
    grads = pl.pallas_call(
        grad_kernel,
        name="weight_grads",
        grid=(n,),
        out_shape=(up_shape, up_shape, down_shape) * 2,
        in_specs=[
            pl.BlockSpec((1, 1024, 1024 // n), lambda i: (0, 0, i)),
            pl.BlockSpec((1, 1024, 1024), lambda i: (1, 0, 0)),
            pl.BlockSpec((1024, 512 // n), lambda i: (0, i)),
            pl.BlockSpec((1024, 512), lambda i: (0, 1)),
            pl.BlockSpec((1024, 512), lambda i: (0, 2)),
            wide, wide, tall, wide_keep, wide_keep, tall_keep,
        ],
        out_specs=(wide, wide, tall) * 2,
        compiler_params=pltpu.CompilerParams(vmem_limit_bytes=48 * 2**20),
    )(tc, tc, act, act, act, gate_w, up_w, down_w, gate_k, up_k, down_k)
    return (out, *grads)


def solution(mesh):
    return jax.shard_map(
        on_device,
        mesh=mesh,
        in_specs=(
            P("tok", "row"),
            P("tok", "row"),
            P("row", ("tok", "col")),
            P("row", ("tok", "col")),
            P(("tok", "col"), "row"),
            P("row", ("tok", "col")),
            P("row", ("tok", "col")),
            P(("tok", "col"), "row"),
        ),
        out_specs=(
            P("tok", "row"),
            P("row", ("tok", "col")),
            P("row", ("tok", "col")),
            P(("tok", "col"), "row"),
            P("row", ("tok", "col")),
            P("row", ("tok", "col")),
            P(("tok", "col"), "row"),
        ),
        check_vma=False,
    )
```

```python
import functools

import jax
import jax.numpy as jnp
from jax import lax
from jax.experimental import pallas as pl
from jax.experimental.pallas import tpu as pltpu
from jax.sharding import PartitionSpec as P

MESH = pl.DeviceIdType.MESH
BF = jnp.bfloat16
F32 = jnp.float32
NCH = 8
T = 128
H = 16
ORDER = (
    ("az", 3), ("az", 2), ("mask", 0), ("s1", 1), ("az", 4), ("ax", 3), ("ax", 2), ("s2", 1), ("az", 6),
    ("s1", 0), ("ax", 4), ("ac", 3), ("az", 7), ("az", 5), ("s2", 0), ("s1", 3), ("ac", 2), ("ax", 6),
    ("s1", 2), ("s3", 0), ("ac", 4), ("s3", 1), ("s2", 3), ("ax", 7), ("s1", 4), ("s2", 2), ("ac", 6),
    ("s3", 3), ("s2", 4), ("s4", 0), ("ac", 7), ("s1", 6), ("ax", 5), ("s3", 4), ("s1", 7), ("s3", 2),
    ("s2", 6), ("s4", 3), ("s5", 0), ("ac", 5), ("s4", 4), ("s3", 6), ("s1", 5), ("s2", 7), ("s5", 3),
    ("s4", 2), ("s5", 4), ("s2", 5), ("s3", 7), ("s6", 3), ("s4", 6), ("s6", 4), ("s5", 2), ("s3", 5),
    ("s4", 7), ("s7", 3), ("s5", 6), ("s7", 4), ("s7b", 3), ("s6", 2), ("s4", 5), ("s6", 6), ("s7", 2),
    ("s5", 7), ("s7b", 4), ("s4", 1), ("s7b", 2), ("s5", 5), ("s8", 3), ("s6", 7), ("s7", 6), ("s8", 4),
    ("s6", 0), ("s6", 5), ("s7b", 6), ("s7", 7), ("s5", 1), ("s7", 0), ("s8", 2), ("s7b", 7), ("s7", 5),
    ("s8", 6), ("s6", 1), ("s7b", 0), ("s7b", 5), ("s8", 7), ("s7", 1), ("g", 1), ("s8", 5), ("s7b", 1),
    ("g", 0), ("s8", 0), ("s9", 0), ("s8", 1), ("s9", 1), ("g", 2),
)


def unpack(keep_ref, i, shifts):
    row = jnp.broadcast_to(keep_ref[pl.ds(i, 1), :], shifts.shape)
    return (jnp.right_shift(row, shifts) & 1).astype(F32)


def for_row_groups(keep_ref, body):
    shifts = lax.broadcasted_iota(jnp.int32, (16, keep_ref.shape[1]), 0)

    def one(i, _):
        body(pl.ds(pl.multiple_of(i * 16, 16), 16), unpack(keep_ref, i, shifts))
        return 0

    lax.fori_loop(0, keep_ref.shape[0], one, 0, unroll=4)


def apply_mask(w_ref, keep_ref, eff_ref):
    def body(at, bits):
        eff_ref[at, :] = (w_ref[at, :].astype(F32) * bits).astype(BF)

    for_row_groups(keep_ref, body)


def finish(full_ref, w_ref, keep_ref, grad_ref, score_ref):
    def body(at, bits):
        full = full_ref[at, :]
        grad_ref[at, :] = (full * bits).astype(BF)
        score_ref[at, :] = (-(w_ref[at, :].astype(F32) * full)).astype(BF)

    for_row_groups(keep_ref, body)


def comm_kernel(
    tokens, cot, gate_w, up_w, down_w, gate_k, up_k, down_k,
    obuf, gate_g, up_g, down_g, gate_s, up_s, down_s,
    tc, gr, ur, dr_w, gw, uw, dw, gk, uk, dk, pre, pre32, rx1, acc, rx3, hs, hr, keep, act,
    dpart, d32, dk32, dr, zown, zs, zr, full, tall,
    ld_sem, send_sem, az, ax, ac, s1, s3, hrs, gh, gy, dks, drs, zrs, ors,
):
    t = lax.axis_index("tok")
    r = lax.axis_index("row")
    c = lax.axis_index("col")
    y, h = r // 2, r % 2
    x, k = c // 2, c % 2
    y_next, y_prev, y_opp = (y + 1) % 4, (y + 3) % 4, (y + 2) % 4
    at_next, at_prev = (t, y_next * 2 + h, c), (t, y_prev * 2 + h, c)
    at_twin = (t, y * 2 + (1 - h), c)
    at_core = (t, r, x * 2 + (1 - k))

    def tok_xor(n):
        return (t % 2 + n % 2) % 2 + 2 * ((t // 2 + n // 2) % 2)

    mine = pl.ds(pl.multiple_of(t * 256, 256), 256)
    loads = [
        pltpu.make_async_copy(src, dst, ld_sem.at[n])
        for n, (src, dst) in enumerate(
            (
                (tokens, tc.at[0, mine]), (cot, tc.at[1, mine]),
                (gate_k, gk), (gate_w, gr), (up_k, uk), (up_w, ur),
                (down_k, dk), (down_w, dr_w),
            )
        )
    ]
    for copy in loads:
        copy.start()

    barrier = pltpu.get_barrier_semaphore()
    peers = [at_next, at_prev, at_twin]
    peers += [(t, r, (c + n) % 8) for n in range(1, 8)]
    peers += [(tok_xor(n), r, c) for n in range(1, 4)]
    for peer in peers:
        pl.semaphore_signal(barrier, inc=1, device_id=peer, device_id_type=MESH)

    SEND = dict(az=0, ax=1, ac=2, rs=3, ag=4, d=5, z=6, o=7, dk=8)

    def send(src, dst, cls, recv, peer):
        pltpu.make_async_remote_copy(
            src_ref=src, dst_ref=dst, send_sem=send_sem.at[SEND[cls]], recv_sem=recv,
            device_id=peer, device_id_type=MESH,
        ).start()

    def wait(ref, sem):
        pltpu.make_async_copy(ref, ref, sem).wait()

    def base(i):
        return tok_xor(i // 2) * 256 + (i % 2) * T

    def rows(i, q, n=H):
        return pl.ds(pl.multiple_of(base(i) + q * n, n), n)

    def stage_az(i):
        at = pl.ds(pl.multiple_of(t * 256 + (i % 2) * T + x * 32, 32), 32)
        send(tc.at[k, at], tc.at[k, at], "az", az.at[i], (tok_xor(i // 2), r, c))

    def stage_ax(i):
        if i < 2:
            return
        at = rows(i, x, 32)
        wait(tc.at[k, at], az.at[i])
        for n in (1, 3, 2):
            send(tc.at[k, at], tc.at[k, at], "ax", ax.at[i], (t, r, ((x + n) % 4) * 2 + k))

    def stage_ac(i):
        if i < 2:
            return
        wait(tc.at[k, pl.ds(0, 96)], ax.at[i])
        at = rows(i, 0, T)
        send(tc.at[k, at], tc.at[k, at], "ac", ac.at[i], at_core)

    def stage_s1(i):
        at = rows(i, 0, T)
        if i >= 2:
            wait(tc.at[1 - k, at], ac.at[i])
        tok_rows = tc[0, at, :]
        cot_rows = tc[1, at, :]
        parts = (
            jnp.dot(tok_rows, gw[...], preferred_element_type=F32),
            jnp.dot(tok_rows, uw[...], preferred_element_type=F32),
            lax.dot_general(
                cot_rows, dw[...], (((1,), (1,)), ((), ())), preferred_element_type=F32
            ),
        )
        for n, part in enumerate(parts):
            pre32[at, pl.ds(n * 512, 512)] = part
            pre[at, pl.ds(n * 512, 512)] = part.astype(BF)
        send(pre.at[rows(i, y_opp * 2)], rx1.at[i, 0], "rs", s1.at[i], at_next)
        send(pre.at[rows(i, y_opp * 2 + 1)], rx1.at[i, 1], "rs", s1.at[i], at_prev)
        send(pre.at[rows(i, y_next * 2 + 1)], rx3.at[i, 0], "rs", s3.at[i], at_next)
        send(pre.at[rows(i, y_prev * 2)], rx3.at[i, 1], "rs", s3.at[i], at_prev)

    def stage_s2(i):
        wait(rx1.at[i], s1.at[i])
        acc[i, 0] = (rx1[i, 0].astype(F32) + pre32[rows(i, y_next * 2), :]).astype(BF)
        send(acc.at[i, 0], rx3.at[i, 2], "rs", s3.at[i], at_next)
        acc[i, 1] = (rx1[i, 1].astype(F32) + pre32[rows(i, y_prev * 2 + 1), :]).astype(BF)
        send(acc.at[i, 1], rx3.at[i, 3], "rs", s3.at[i], at_prev)

    def stage_s3(i):
        wait(rx3.at[i], s3.at[i])

        def total(half):
            return (
                pre32[rows(i, y * 2 + half), :]
                + rx3[i, 1 - half].astype(F32)
                + rx3[i, 2 + half].astype(F32)
            )

        hs[i] = total(1 - h).astype(BF)
        send(hs.at[i], hr.at[i], "rs", hrs.at[i], at_twin)
        keep[i] = total(h)

    def stage_s4(i):
        wait(hr.at[i], hrs.at[i])
        sums = keep[i] + hr[i].astype(F32)
        gate, up, back = sums[:, :512], sums[:, 512:1024], sums[:, 1024:]
        sig = jax.nn.sigmoid(gate)
        silu = gate * sig
        at = rows(i, r)
        act[at, pl.ds(0, 512)] = (silu * up).astype(BF)
        act[at, pl.ds(512, 512)] = (back * up * (sig * (1.0 + gate * (1.0 - sig)))).astype(BF)
        act[at, pl.ds(1024, 512)] = (back * silu).astype(BF)
        send(act.at[at], act.at[at], "ag", gh.at[i], at_twin)
        send(act.at[at], act.at[at], "ag", gy.at[i, h], at_next)
        send(act.at[at], act.at[at], "ag", gy.at[i, 1 - h], at_prev)

    def stage_s5(i):
        at = rows(i, y * 2 + (1 - h))
        wait(act.at[at], gh.at[i])
        send(act.at[at], act.at[at], "ag", gy.at[i, 1 - h], at_next)
        send(act.at[at], act.at[at], "ag", gy.at[i, h], at_prev)

    def stage_s6(i):
        wait(act.at[pl.ds(0, 2 * H)], gy.at[i, 0])
        at = rows(i, y_prev * 2)
        send(act.at[at], act.at[at], "ag", gy.at[i, 1], at_next)
        at = rows(i, y_next * 2 + 1)
        send(act.at[at], act.at[at], "ag", gy.at[i, 1], at_prev)

    def stage_s7(i):
        wait(act.at[pl.ds(0, 4 * H)], gy.at[i, 1])
        at = rows(i, 0, T)
        nt = (((1,), (1,)), ((), ()))
        part = lax.dot_general(
            act[at, pl.ds(512, 512)], gw[...], nt, preferred_element_type=F32
        ) + lax.dot_general(
            act[at, pl.ds(1024, 512)], uw[...], nt, preferred_element_type=F32
        )
        d32[i] = part
        other = pl.ds(pl.multiple_of((1 - k) * 64, 64), 64)
        send(d32.at[i, other], dk32.at[i], "dk", dks.at[i], at_core)

    def stage_s7b(i):
        wait(dk32.at[i], dks.at[i])
        own = pl.ds(pl.multiple_of(k * 64, 64), 64)
        part = d32[i, own, :] + dk32[i]
        dk32[i] = part
        dpart[i] = part.astype(BF)
        for n in (1, 3, 2):
            peer = (x + n) % 4
            at = pl.ds(pl.multiple_of(peer * H, H), H)
            send(dpart.at[i, at], dr.at[i, n - 1], "d", drs.at[i], (t, r, peer * 2 + k))

    def stage_s8(i):
        wait(dr.at[i], drs.at[i])
        total = dk32[i, pl.ds(pl.multiple_of(x * H, H), H), :]
        for n in range(3):
            total = total + dr[i, n].astype(F32)
        if i < 2:
            zown[i] = total
        else:
            zs[i - 2] = total
            send(zs.at[i - 2], zr.at[i - 2], "z", zrs.at[i - 2], (tok_xor(i // 2), r, c))

    def stage_s9(u):
        total = zown[u]
        for n in range(3):
            wait(zr.at[2 * n + u], zrs.at[2 * n + u])
            total = total + zr[2 * n + u]
        at = pl.ds(pl.multiple_of(u * T + (k * 4 + x) * H, H), H)
        obuf[at, :] = total.astype(BF)
        for n in range(7):
            send(obuf.at[at], obuf.at[at], "o", ors.at[u], (t, r, (c + n + 1) % 8))

    tn = (((0,), (0,)), ((), ()))

    def stage_g(n):
        if n == 2:
            tall[...] = lax.dot_general(
                act[:, pl.ds(0, 512)], tc[1], tn, preferred_element_type=F32
            )
            finish(tall, dr_w, dk, down_g, down_s)
            return
        full[...] = lax.dot_general(
            tc[0], act[:, pl.ds(512 * (n + 1), 512)], tn, preferred_element_type=F32
        )
        if n == 0:
            finish(full, gr, gk, gate_g, gate_s)
        else:
            finish(full, ur, uk, up_g, up_s)

    def stage_mask(_):
        for n, (w, kk, eff) in enumerate(((gr, gk, gw), (ur, uk, uw), (dr_w, dk, dw))):
            loads[2 + 2 * n].wait()
            loads[3 + 2 * n].wait()
            apply_mask(w, kk, eff)

    loads[0].wait()
    loads[1].wait()
    pl.semaphore_wait(barrier, len(peers))
    stages = dict(
        az=stage_az, mask=stage_mask, ax=stage_ax, ac=stage_ac, s1=stage_s1, s2=stage_s2,
        s3=stage_s3, s4=stage_s4, s5=stage_s5, s6=stage_s6, s7=stage_s7, s7b=stage_s7b,
        s8=stage_s8, s9=stage_s9, g=stage_g,
    )
    for name, i in ORDER:
        stages[name](i)
    for u in range(2):
        wait(obuf.at[pl.ds(0, 7 * H)], ors.at[u])
    wait(tc.at[0, pl.ds(0, 6 * 32)], send_sem.at[0])
    wait(tc.at[0, pl.ds(0, 18 * 32)], send_sem.at[1])
    wait(tc.at[0, pl.ds(0, 6 * T)], send_sem.at[2])
    wait(pre.at[pl.ds(0, 56 * H)], send_sem.at[3])
    wait(act.at[pl.ds(0, 56 * H)], send_sem.at[4])
    wait(dpart.at[pl.ds(0, 6)], send_sem.at[5])
    wait(zs, send_sem.at[6])
    wait(obuf.at[pl.ds(0, 14 * H)], send_sem.at[7])
    wait(dk32, send_sem.at[8])


def store_kernel(*refs):
    n = len(refs) // 2
    sems = refs[-1]
    copies = [
        pltpu.make_async_copy(refs[i], refs[n + i], sems.at[i]) for i in range(n)
    ]
    for copy in copies:
        copy.start()
    for copy in copies:
        copy.wait()


def on_device(*args):
    hbm = pl.BlockSpec(memory_space=pltpu.HBM)
    vmem = pl.BlockSpec(memory_space=pltpu.VMEM)
    dma = pltpu.SemaphoreType.DMA
    shapes = ((256, 1024),) + ((1024, 512), (1024, 512), (512, 1024)) * 2
    args = [pltpu.with_memory_space_constraint(a, pltpu.HBM) for a in args]
    outs = pl.pallas_call(
        comm_kernel,
        name="exchange",
        out_shape=[pltpu.VMEM(s, BF) for s in shapes],
        in_specs=[hbm] * 8,
        out_specs=[vmem] * 7,
        scratch_shapes=[
            pltpu.VMEM((2, 1024, 1024), BF),
            pltpu.VMEM((1024, 512), BF),
            pltpu.VMEM((1024, 512), BF),
            pltpu.VMEM((512, 1024), BF),
            pltpu.VMEM((1024, 512), BF),
            pltpu.VMEM((1024, 512), BF),
            pltpu.VMEM((512, 1024), BF),
            pltpu.VMEM((64, 512), jnp.int32),
            pltpu.VMEM((64, 512), jnp.int32),
            pltpu.VMEM((32, 1024), jnp.int32),
            pltpu.VMEM((1024, 1536), BF),
            pltpu.VMEM((1024, 1536), F32),
            pltpu.VMEM((NCH, 2, H, 1536), BF),
            pltpu.VMEM((NCH, 2, H, 1536), BF),
            pltpu.VMEM((NCH, 4, H, 1536), BF),
            pltpu.VMEM((NCH, H, 1536), BF),
            pltpu.VMEM((NCH, H, 1536), BF),
            pltpu.VMEM((NCH, H, 1536), F32),
            pltpu.VMEM((1024, 1536), BF),
            pltpu.VMEM((NCH, 64, 1024), BF),
            pltpu.VMEM((NCH, T, 1024), F32),
            pltpu.VMEM((NCH, 64, 1024), F32),
            pltpu.VMEM((NCH, 3, H, 1024), BF),
            pltpu.VMEM((2, H, 1024), F32),
            pltpu.VMEM((6, H, 1024), F32),
            pltpu.VMEM((6, H, 1024), F32),
            pltpu.VMEM((1024, 512), F32),
            pltpu.VMEM((512, 1024), F32),
            dma((8,)),
            dma((9,)),
            dma((NCH,)),
            dma((NCH,)),
            dma((NCH,)),
            dma((NCH,)),
            dma((NCH,)),
            dma((NCH,)),
            dma((NCH,)),
            dma((NCH, 2)),
            dma((NCH,)),
            dma((NCH,)),
            dma((6,)),
            dma((2,)),
        ],
        compiler_params=pltpu.CompilerParams(
            collective_id=0, has_side_effects=True, vmem_limit_bytes=50 * 2**20
        ),
    )(*args)
    return tuple(
        pl.pallas_call(
            store_kernel,
            name="store",
            out_shape=[jax.ShapeDtypeStruct(s, BF) for s in shapes],
            in_specs=[vmem] * 7,
            out_specs=[hbm] * 7,
            scratch_shapes=[dma((7,))],
            compiler_params=pltpu.CompilerParams(vmem_limit_bytes=2**20),
        )(*[pltpu.with_memory_space_constraint(o, pltpu.VMEM) for o in outs])
    )


def solution(mesh):
    return jax.shard_map(
        on_device,
        mesh=mesh,
        in_specs=(
            P("tok", "row"),
            P("tok", "row"),
            P("row", ("tok", "col")),
            P("row", ("tok", "col")),
            P(("tok", "col"), "row"),
            P("row", ("tok", "col")),
            P("row", ("tok", "col")),
            P(("tok", "col"), "row"),
        ),
        out_specs=(
            P("tok", "row"),
            P("row", ("tok", "col")),
            P("row", ("tok", "col")),
            P(("tok", "col"), "row"),
            P("row", ("tok", "col")),
            P("row", ("tok", "col")),
            P(("tok", "col"), "row"),
        ),
        check_vma=False,
    )
```

```python
import functools

import jax
import jax.numpy as jnp
from jax import lax
from jax.experimental import pallas as pl
from jax.experimental.pallas import tpu as pltpu
from jax.sharding import PartitionSpec as P

MESH = pl.DeviceIdType.MESH
BF = jnp.bfloat16
F32 = jnp.float32
NCH = 8
T = 128
H = 16
BLOCK = (0, 0, 1, 2, 2, 3, 3, 1)
HALF = (0, 1, 0, 0, 1, 0, 1, 1)
LAST = NCH - 1
ORDER = (
    ("s1", 0), ("ax", 2), ("s1", 1), ("ax", 3), ("s2", 0), ("ac", 2), ("ax", 4), ("s1", 2), ("s2", 1),
    ("s3", 0), ("ax", 5), ("ac", 3), ("s2", 2), ("s1", 3), ("ax", 6), ("ax", 7), ("ac", 4), ("s3", 1),
    ("s4", 0), ("ac", 5), ("s3", 2), ("s2", 3), ("s1", 4), ("s1", 5), ("ac", 6), ("s3", 3), ("s2", 4),
    ("s1", 6), ("ac", 7), ("s2", 5), ("s4", 2), ("s5", 0), ("s3", 4), ("s2", 6), ("s4", 3), ("s1", 7),
    ("s3", 5), ("s6", 0), ("s5", 2), ("s3", 6), ("s2", 7), ("s5", 3), ("s4", 4), ("s4", 5), ("s7", 0),
    ("s6", 2), ("s3", 7), ("s6", 3), ("s4", 6), ("s7b", 0), ("s5", 4), ("s4", 1), ("s7", 2), ("s5", 5),
    ("s7", 3), ("s6", 4), ("t4", 1), ("s7b", 2), ("s4", 7), ("s7b", 3), ("s5", 6), ("s6", 5), ("s7", 4),
    ("t4", 5), ("t4", 4), ("t4", 2), ("s6", 6), ("s7b", 4), ("s5", 7), ("s7", 5), ("s5", 1), ("t4", 0),
    ("s7", 6), ("s6", 7), ("s7b", 5), ("t5", 1), ("s8", 0), ("t4", 6), ("s6", 1), ("s8", 2), ("t4", 7),
    ("s7b", 6), ("t4", 3), ("s7", 7), ("s8", 3), ("s7", 1), ("t5", 2), ("s7b", 7), ("s8", 5), ("t5", 5),
    ("t5", 6), ("t5", 7), ("s7b", 1), ("s8", 4), ("t5", 3), ("t5", 0), ("t5", 4), ("t6", 1), ("s8", 6),
    ("s8", 7), ("s9", 0), ("t7", 1), ("t6", 2), ("t6", 5), ("t6", 7), ("t6", 3), ("t6", 6), ("t6", 0),
    ("t6", 4), ("s8", 1), ("s9", 1), ("t7", 2), ("g", 1), ("t7", 6), ("t7", 0), ("t7", 3), ("g", 0),
    ("t7", 7), ("t7", 5), ("t7", 4), ("g", 2),
)


def unpack(keep_ref, i, shifts):
    row = jnp.broadcast_to(keep_ref[pl.ds(i, 1), :], shifts.shape)
    return (jnp.right_shift(row, shifts) & 1).astype(F32)


def for_row_groups(keep_ref, body):
    shifts = lax.broadcasted_iota(jnp.int32, (16, keep_ref.shape[1]), 0)

    def one(i, _):
        body(pl.ds(pl.multiple_of(i * 16, 16), 16), unpack(keep_ref, i, shifts))
        return 0

    lax.fori_loop(0, keep_ref.shape[0], one, 0, unroll=4)


def apply_mask(w_ref, keep_ref, eff_ref):
    def body(at, bits):
        eff_ref[at, :] = (w_ref[at, :].astype(F32) * bits).astype(BF)

    for_row_groups(keep_ref, body)


def finish(full_ref, w_ref, keep_ref, grad_ref, score_ref):
    def body(at, bits):
        full = full_ref[at, :]
        grad_ref[at, :] = (full * bits).astype(BF)
        score_ref[at, :] = (-(w_ref[at, :].astype(F32) * full)).astype(BF)

    for_row_groups(keep_ref, body)


def comm_kernel(
    tokens, cot, gate_w, up_w, down_w, gate_k, up_k, down_k,
    obuf, gate_g, up_g, down_g, gate_s, up_s, down_s,
    tc, gr, ur, dr_w, gw, uw, dw, gk, uk, dk, pre, pre32, rx1, acc, rx3, hs, hr, keep, act, hid,
    dpart, d32, dk32, dr, dr_last, zown, zs, zr, zs_last, zr_last, full, tall,
    ld_sem, send_sem, az, ax, ac, s1, s3, hrs, gh, gy, th, ty, dks, drs, zrs, ors,
):
    t = lax.axis_index("tok")
    r = lax.axis_index("row")
    c = lax.axis_index("col")
    rem = lax.rem
    h, k = rem(r, 2), rem(c, 2)
    y, x = lax.div(r, 2), lax.div(c, 2)
    y_next, y_prev, y_opp = rem(y + 1, 4), rem(y + 3, 4), rem(y + 2, 4)
    x_of = [rem(x + n, 4) for n in range(4)]
    x_col = [at_x * 2 + k for at_x in x_of]
    col_of = [rem(c + n, 8) for n in range(8)]
    at_next, at_prev = (t, y_next * 2 + h, c), (t, y_prev * 2 + h, c)
    at_twin = (t, y * 2 + (1 - h), c)
    at_core = (t, r, x * 2 + (1 - k))

    t0, t1 = rem(t, 2), lax.div(t, 2)
    tok_of = [rem(t0 + n % 2, 2) + 2 * rem(t1 + n // 2, 2) for n in range(4)]
    base_of = [[pl.multiple_of(b * 256 + u * T, T) for u in range(2)] for b in tok_of]

    mine = pl.ds(pl.multiple_of(t * 256, 256), 256)
    loads = [
        pltpu.make_async_copy(src, dst, ld_sem.at[n])
        for n, (src, dst) in enumerate(
            (
                (tokens, tc.at[0, mine]), (cot, tc.at[1, mine]),
                (gate_k, gk), (gate_w, gr), (up_k, uk), (up_w, ur),
                (down_k, dk), (down_w, dr_w),
            )
        )
    ]
    for copy in loads:
        copy.start()

    barrier = pltpu.get_barrier_semaphore()
    peers = [at_next, at_prev, at_twin]
    peers += [(t, r, col_of[n]) for n in range(1, 8)]
    peers += [(tok_of[n], r, c) for n in range(1, 4)]
    for peer in peers:
        pl.semaphore_signal(barrier, inc=1, device_id=peer, device_id_type=MESH)

    SEND = dict(az=0, ax=1, ac=2, rs=3, ag=4, d=5, z=6, o=7, dk=8, dl=9, zl=10, t=11)

    def send(src, dst, cls, recv, peer):
        pltpu.make_async_remote_copy(
            src_ref=src, dst_ref=dst, send_sem=send_sem.at[SEND[cls]], recv_sem=recv,
            device_id=peer, device_id_type=MESH,
        ).start()

    def wait(ref, sem):
        pltpu.make_async_copy(ref, ref, sem).wait()

    def base(i):
        return base_of[BLOCK[i]][HALF[i]]

    def rows(i, q, n=H):
        return pl.ds(pl.multiple_of(base(i) + q * n, n), n)

    def stage_az(i):
        for n in (0, 2) if BLOCK[i] == 1 else (0,):
            start = base_of[0][HALF[i]] + x_of[n] * 32
            at = pl.ds(pl.multiple_of(start, 32), 32)
            send(tc.at[k, at], tc.at[k, at], "az", az.at[i], (tok_of[BLOCK[i]], r, c))

    def stage_ax(i):
        near = BLOCK[i] == 1
        at = rows(i, x, 32)
        wait(tc.at[k, pl.ds(0, 64 if near else 32)], az.at[i])
        for n in (1, 3) if near else (1, 3, 2):
            send(tc.at[k, at], tc.at[k, at], "ax", ax.at[i], (t, r, x_col[n]))

    def stage_ac(i):
        wait(tc.at[k, pl.ds(0, 64 if BLOCK[i] == 1 else 96)], ax.at[i])
        at = rows(i, 0, T)
        send(tc.at[k, at], tc.at[k, at], "ac", ac.at[i], at_core)

    def forward(i, n):
        at = rows(i, 0, T)
        if n == 2:
            part = lax.dot_general(
                tc[1, at, :], dw[...], (((1,), (1,)), ((), ())), preferred_element_type=F32
            )
        else:
            part = jnp.dot(tc[0, at, :], (gw, uw)[n][...], preferred_element_type=F32)
        pre32[at, pl.ds(n * 512, 512)] = part
        pre[at, pl.ds(n * 512, 512)] = part.astype(BF)

    def stage_s1(i):
        if BLOCK[i]:
            wait(tc.at[1 - k, rows(i, 0, T)], ac.at[i])
        if i:
            for n in range(3):
                forward(i, n)
        send(pre.at[rows(i, y_opp * 2)], rx1.at[i, 0], "rs", s1.at[i], at_next)
        send(pre.at[rows(i, y_opp * 2 + 1)], rx1.at[i, 1], "rs", s1.at[i], at_prev)
        send(pre.at[rows(i, y_next * 2 + 1)], rx3.at[i, 0], "rs", s3.at[i], at_next)
        send(pre.at[rows(i, y_prev * 2)], rx3.at[i, 1], "rs", s3.at[i], at_prev)

    def stage_s2(i):
        wait(rx1.at[i], s1.at[i])
        acc[i, 0] = (rx1[i, 0].astype(F32) + pre32[rows(i, y_next * 2), :]).astype(BF)
        send(acc.at[i, 0], rx3.at[i, 2], "rs", s3.at[i], at_next)
        acc[i, 1] = (rx1[i, 1].astype(F32) + pre32[rows(i, y_prev * 2 + 1), :]).astype(BF)
        send(acc.at[i, 1], rx3.at[i, 3], "rs", s3.at[i], at_prev)

    def stage_s3(i):
        wait(rx3.at[i], s3.at[i])

        def total(half):
            return (
                pre32[rows(i, y * 2 + half), :]
                + rx3[i, 1 - half].astype(F32)
                + rx3[i, 2 + half].astype(F32)
            )

        hs[i] = total(1 - h).astype(BF)
        send(hs.at[i], hr.at[i], "rs", hrs.at[i], at_twin)
        keep[i] = total(h)

    def stage_s4(i):
        wait(hr.at[i], hrs.at[i])
        sums = keep[i] + hr[i].astype(F32)
        gate, up, back = sums[:, :512], sums[:, 512:1024], sums[:, 1024:]
        sig = jax.nn.sigmoid(gate)
        silu = gate * sig
        at = rows(i, r)
        hid[at, :] = (silu * up).astype(BF)
        act[at, pl.ds(0, 512)] = (back * up * (sig * (1.0 + gate * (1.0 - sig)))).astype(BF)
        act[at, pl.ds(512, 512)] = (back * silu).astype(BF)
        gather_own(i, act, "ag", gh, gy)

    def gather_own(i, ref, cls, twin_sem, ring_sem):
        at = rows(i, r)
        send(ref.at[at], ref.at[at], cls, twin_sem.at[i], at_twin)
        send(ref.at[at], ref.at[at], cls, ring_sem.at[i, h], at_next)
        send(ref.at[at], ref.at[at], cls, ring_sem.at[i, 1 - h], at_prev)

    def gather_twin(i, ref, cls, twin_sem, ring_sem):
        at = rows(i, y * 2 + (1 - h))
        wait(ref.at[at], twin_sem.at[i])
        send(ref.at[at], ref.at[at], cls, ring_sem.at[i, 1 - h], at_next)
        send(ref.at[at], ref.at[at], cls, ring_sem.at[i, h], at_prev)

    def gather_far(i, ref, cls, ring_sem):
        wait(ref.at[pl.ds(0, 2 * H)], ring_sem.at[i, 0])
        at = rows(i, y_prev * 2)
        send(ref.at[at], ref.at[at], cls, ring_sem.at[i, 1], at_next)
        at = rows(i, y_next * 2 + 1)
        send(ref.at[at], ref.at[at], cls, ring_sem.at[i, 1], at_prev)

    def stage_s5(i):
        gather_twin(i, act, "ag", gh, gy)

    def stage_s6(i):
        gather_far(i, act, "ag", gy)

    def stage_t4(i):
        gather_own(i, hid, "t", th, ty)

    def stage_t5(i):
        gather_twin(i, hid, "t", th, ty)

    def stage_t6(i):
        gather_far(i, hid, "t", ty)

    def stage_t7(i):
        wait(hid.at[pl.ds(0, 4 * H)], ty.at[i, 1])

    def stage_s7(i):
        wait(act.at[pl.ds(0, 4 * H)], gy.at[i, 1])
        at = rows(i, 0, T)
        nt = (((1,), (1,)), ((), ()))
        part = lax.dot_general(
            act[at, pl.ds(0, 512)], gw[...], nt, preferred_element_type=F32
        ) + lax.dot_general(
            act[at, pl.ds(512, 512)], uw[...], nt, preferred_element_type=F32
        )
        d32[i] = part
        other = pl.ds(pl.multiple_of((1 - k) * 64, 64), 64)
        send(d32.at[i, other], dk32.at[i], "dk", dks.at[i], at_core)

    def stage_s7b(i):
        wait(dk32.at[i], dks.at[i])
        own = pl.ds(pl.multiple_of(k * 64, 64), 64)
        part = d32[i, own, :] + dk32[i]
        dk32[i] = part
        if i == LAST:
            dpart[...] = part.astype(BF)
        for n in (1, 3, 2):
            at = pl.ds(pl.multiple_of(x_of[n] * H, H), H)
            to = (t, r, x_col[n])
            if i == LAST:
                send(dpart.at[at], dr_last.at[n - 1], "dl", drs.at[i], to)
            else:
                send(dk32.at[i, at], dr.at[i, n - 1], "d", drs.at[i], to)

    def stage_s8(i):
        came = dr_last if i == LAST else dr.at[i]
        wait(came, drs.at[i])
        total = dk32[i, pl.ds(pl.multiple_of(x * H, H), H), :]
        for n in range(3):
            total = total + came[n].astype(F32)
        b, u = BLOCK[i], HALF[i]
        if b == 0:
            zown[u] = total
        elif i == LAST:
            zs_last[...] = total
            send(zs_last, zr_last, "zl", zrs.at[u, b], (tok_of[b], r, c))
        else:
            zs[u, b] = total.astype(BF)
            send(zs.at[u, b], zr.at[u, b], "z", zrs.at[u, b], (tok_of[b], r, c))

    def stage_s9(u):
        total = zown[u]
        for b in range(1, 4):
            came = zr_last if (b, u) == (BLOCK[LAST], HALF[LAST]) else zr.at[u, b]
            wait(came, zrs.at[u, b])
            total = total + came[...].astype(F32)
        at = pl.ds(pl.multiple_of(u * T + (k * 4 + x) * H, H), H)
        obuf[at, :] = total.astype(BF)
        for n in range(7):
            send(obuf.at[at], obuf.at[at], "o", ors.at[u], (t, r, col_of[n + 1]))

    tn = (((0,), (0,)), ((), ()))

    def stage_g(n):
        if n == 2:
            tall[...] = lax.dot_general(
                hid[...], tc[1], tn, preferred_element_type=F32
            )
            finish(tall, dr_w, dk, down_g, down_s)
            return
        full[...] = lax.dot_general(
            tc[0], act[:, pl.ds(512 * n, 512)], tn, preferred_element_type=F32
        )
        if n == 0:
            finish(full, gr, gk, gate_g, gate_s)
        else:
            finish(full, ur, uk, up_g, up_s)

    def prepare(n):
        loads[2 + 2 * n].wait()
        loads[3 + 2 * n].wait()
        apply_mask((gr, ur, dr_w)[n], (gk, uk, dk)[n], (gw, uw, dw)[n])
        forward(0, n)

    loads[0].wait()
    loads[1].wait()
    prepare(0)
    pl.semaphore_wait(barrier, len(peers))
    for i in range(NCH):
        if BLOCK[i]:
            stage_az(i)
    prepare(1)
    prepare(2)
    stages = dict(
        ax=stage_ax, ac=stage_ac, s1=stage_s1, s2=stage_s2, s3=stage_s3, s4=stage_s4,
        s5=stage_s5, s6=stage_s6, s7=stage_s7, s7b=stage_s7b, s8=stage_s8, t4=stage_t4,
        t5=stage_t5, t6=stage_t6, t7=stage_t7, s9=stage_s9, g=stage_g,
    )
    for name, i in ORDER:
        stages[name](i)
    for u in range(2):
        wait(obuf.at[pl.ds(0, 7 * H)], ors.at[u])
    wait(tc.at[0, pl.ds(0, 8 * 32)], send_sem.at[0])
    wait(tc.at[0, pl.ds(0, 16 * 32)], send_sem.at[1])
    wait(tc.at[0, pl.ds(0, 6 * T)], send_sem.at[2])
    wait(pre.at[pl.ds(0, 56 * H)], send_sem.at[3])
    wait(act.at[pl.ds(0, 56 * H)], send_sem.at[4])
    wait(dr, send_sem.at[5])
    n_far = sum(1 for i in range(LAST) if BLOCK[i])
    wait(obuf.at[pl.ds(0, n_far * H)], send_sem.at[6])
    wait(obuf.at[pl.ds(0, 14 * H)], send_sem.at[7])
    wait(dk32, send_sem.at[8])
    wait(dr_last, send_sem.at[9])
    if BLOCK[LAST]:
        wait(zs_last, send_sem.at[10])
    wait(hid.at[pl.ds(0, 56 * H)], send_sem.at[11])


def store_kernel(*refs):
    n = len(refs) // 2
    sems = refs[-1]
    copies = [
        pltpu.make_async_copy(refs[i], refs[n + i], sems.at[i]) for i in range(n)
    ]
    for copy in copies:
        copy.start()
    for copy in copies:
        copy.wait()


def on_device(*args):
    hbm = pl.BlockSpec(memory_space=pltpu.HBM)
    vmem = pl.BlockSpec(memory_space=pltpu.VMEM)
    dma = pltpu.SemaphoreType.DMA
    shapes = ((256, 1024),) + ((1024, 512), (1024, 512), (512, 1024)) * 2
    args = [pltpu.with_memory_space_constraint(a, pltpu.HBM) for a in args]
    outs = pl.pallas_call(
        comm_kernel,
        name="exchange",
        out_shape=[pltpu.VMEM(s, BF) for s in shapes],
        in_specs=[hbm] * 8,
        out_specs=[vmem] * 7,
        scratch_shapes=[
            pltpu.VMEM((2, 1024, 1024), BF),
            pltpu.VMEM((1024, 512), BF),
            pltpu.VMEM((1024, 512), BF),
            pltpu.VMEM((512, 1024), BF),
            pltpu.VMEM((1024, 512), BF),
            pltpu.VMEM((1024, 512), BF),
            pltpu.VMEM((512, 1024), BF),
            pltpu.VMEM((64, 512), jnp.int32),
            pltpu.VMEM((64, 512), jnp.int32),
            pltpu.VMEM((32, 1024), jnp.int32),
            pltpu.VMEM((1024, 1536), BF),
            pltpu.VMEM((1024, 1536), F32),
            pltpu.VMEM((NCH, 2, H, 1536), BF),
            pltpu.VMEM((NCH, 2, H, 1536), BF),
            pltpu.VMEM((NCH, 4, H, 1536), BF),
            pltpu.VMEM((NCH, H, 1536), BF),
            pltpu.VMEM((NCH, H, 1536), BF),
            pltpu.VMEM((NCH, H, 1536), F32),
            pltpu.VMEM((1024, 1024), BF),
            pltpu.VMEM((1024, 512), BF),
            pltpu.VMEM((64, 1024), BF),
            pltpu.VMEM((NCH, T, 1024), F32),
            pltpu.VMEM((NCH, 64, 1024), F32),
            pltpu.VMEM((LAST, 3, H, 1024), F32),
            pltpu.VMEM((3, H, 1024), BF),
            pltpu.VMEM((2, H, 1024), F32),
            pltpu.VMEM((2, 4, H, 1024), BF),
            pltpu.VMEM((2, 4, H, 1024), BF),
            pltpu.VMEM((H, 1024), F32),
            pltpu.VMEM((H, 1024), F32),
            pltpu.VMEM((1024, 512), F32),
            pltpu.VMEM((512, 1024), F32),
            dma((8,)),
            dma((12,)),
            dma((NCH,)),
            dma((NCH,)),
            dma((NCH,)),
            dma((NCH,)),
            dma((NCH,)),
            dma((NCH,)),
            dma((NCH,)),
            dma((NCH, 2)),
            dma((NCH,)),
            dma((NCH, 2)),
            dma((NCH,)),
            dma((NCH,)),
            dma((2, 4)),
            dma((2,)),
        ],
        compiler_params=pltpu.CompilerParams(
            collective_id=0, has_side_effects=True, vmem_limit_bytes=50 * 2**20
        ),
    )(*args)
    return tuple(
        pl.pallas_call(
            store_kernel,
            name="store",
            out_shape=[jax.ShapeDtypeStruct(s, BF) for s in shapes],
            in_specs=[vmem] * 7,
            out_specs=[hbm] * 7,
            scratch_shapes=[dma((7,))],
            compiler_params=pltpu.CompilerParams(vmem_limit_bytes=2**20),
        )(*[pltpu.with_memory_space_constraint(o, pltpu.VMEM) for o in outs])
    )


def solution(mesh):
    return jax.shard_map(
        on_device,
        mesh=mesh,
        in_specs=(
            P("tok", "row"),
            P("tok", "row"),
            P("row", ("tok", "col")),
            P("row", ("tok", "col")),
            P(("tok", "col"), "row"),
            P("row", ("tok", "col")),
            P("row", ("tok", "col")),
            P(("tok", "col"), "row"),
        ),
        out_specs=(
            P("tok", "row"),
            P("row", ("tok", "col")),
            P("row", ("tok", "col")),
            P(("tok", "col"), "row"),
            P("row", ("tok", "col")),
            P("row", ("tok", "col")),
            P(("tok", "col"), "row"),
        ),
        check_vma=False,
    )
```

```python
import functools

import jax
import jax.numpy as jnp
from jax import lax
from jax.experimental import pallas as pl
from jax.experimental.pallas import tpu as pltpu
from jax.sharding import PartitionSpec as P

MESH = pl.DeviceIdType.MESH
BF = jnp.bfloat16
F32 = jnp.float32
NCH = 8
T = 128
H = 16
BLOCK = (0, 0, 1, 2, 2, 3, 3, 1)
HALF = (0, 1, 0, 0, 1, 0, 1, 1)
WHOLE = (7,)
NARROW = (0, 1, 7,)
ORDER = (
    ("s1", 0), ("s1", 1), ("ax", 2), ("s2", 0), ("ax", 3), ("ac", 2), ("ax", 4), ("s1", 2), ("s3", 0),
    ("ax", 5), ("s2", 1), ("ac", 3), ("s2", 2), ("s1", 3), ("ax", 6), ("s3", 1), ("ac", 4), ("s4", 0),
    ("s3", 2), ("ac", 5), ("s2", 3), ("s1", 4), ("s1", 5), ("s3", 3), ("ac", 6), ("s2", 4), ("s1", 6),
    ("s2", 5), ("s5", 0), ("s4", 2), ("ax", 7), ("s3", 4), ("s2", 6), ("s4", 3), ("ac", 7), ("s3", 5),
    ("s6", 0), ("s5", 2), ("s1", 7), ("s3", 6), ("s5", 3), ("s4", 4), ("s7", 0), ("s2", 7), ("s6", 2),
    ("s4", 5), ("s6", 3), ("s7b", 0), ("s4", 6), ("s3", 7), ("s5", 4), ("s7", 2), ("s5", 5), ("s7", 3),
    ("s7b", 2), ("s6", 4), ("t4", 6), ("s5", 6), ("s4", 1), ("s6", 5), ("t4", 3), ("s7b", 3), ("t4", 1),
    ("s7", 4), ("s6", 6), ("s4", 7), ("t4", 0), ("s7b", 4), ("s7", 5), ("s5", 1), ("s7", 6), ("s7b", 5),
    ("s6", 7), ("t4", 4), ("t4", 5), ("s6", 1), ("t5", 3), ("t4", 7), ("t5", 1), ("s7b", 6), ("t5", 6),
    ("s8", 3), ("s7", 7), ("t4", 2), ("s7", 1), ("s7b", 7), ("s8", 5), ("t5", 4), ("t5", 5), ("s8", 2),
    ("t6", 3), ("t6", 6), ("s8", 4), ("s7b", 1), ("t6", 7), ("t5", 0), ("s8", 6), ("t6", 4), ("t6", 5),
    ("s8", 0), ("t5", 2), ("t6", 1), ("s8", 7), ("s9", 0), ("g", 1), ("t7", 5), ("t7", 7), ("s8", 1),
    ("t7", 6), ("t7", 1), ("s9", 1), ("t7", 4), ("t6", 0), ("t6", 2), ("g", 0), ("t7", 0), ("t7", 3),
    ("t7", 2), ("g", 2),
)


def unpack(keep_ref, i, shifts):
    row = jnp.broadcast_to(keep_ref[pl.ds(i, 1), :], shifts.shape)
    return (jnp.right_shift(row, shifts) & 1).astype(F32)


def for_row_groups(keep_ref, body):
    shifts = lax.broadcasted_iota(jnp.int32, (16, keep_ref.shape[1]), 0)

    def one(i, _):
        body(pl.ds(pl.multiple_of(i * 16, 16), 16), unpack(keep_ref, i, shifts))
        return 0

    lax.fori_loop(0, keep_ref.shape[0], one, 0, unroll=4)


def apply_mask(w_ref, keep_ref, eff_ref):
    def body(at, bits):
        eff_ref[at, :] = (w_ref[at, :].astype(F32) * bits).astype(BF)

    for_row_groups(keep_ref, body)


def finish(full_ref, w_ref, keep_ref, grad_ref, score_ref):
    def body(at, bits):
        full = full_ref[at, :]
        grad_ref[at, :] = (full * bits).astype(BF)
        score_ref[at, :] = (-(w_ref[at, :].astype(F32) * full)).astype(BF)

    for_row_groups(keep_ref, body)


def comm_kernel(
    tokens, cot, gate_w, up_w, down_w, gate_k, up_k, down_k,
    obuf, gate_g, up_g, down_g, gate_s, up_s, down_s,
    tc, gr, ur, dr_w, gw, uw, dw, gk, uk, dk, pre, pre32, rx1, acc, rx3, hs, hr, keep, act, hid,
    dpart, d32, dk32, dr, dr16, zown, zs, zr, zs32, zr32, full, tall,
    ld_sem, send_sem, az, ax, ac, s1, s3, hrs, gh, gy, th, ty, dks, drs, zrs, ors,
):
    t = lax.axis_index("tok")
    r = lax.axis_index("row")
    c = lax.axis_index("col")
    rem = lax.rem
    h, k = rem(r, 2), rem(c, 2)
    y, x = lax.div(r, 2), lax.div(c, 2)
    y_next, y_prev, y_opp = rem(y + 1, 4), rem(y + 3, 4), rem(y + 2, 4)
    x_of = [rem(x + n, 4) for n in range(4)]
    x_col = [at_x * 2 + k for at_x in x_of]
    col_of = [rem(c + n, 8) for n in range(8)]
    at_next, at_prev = (t, y_next * 2 + h, c), (t, y_prev * 2 + h, c)
    at_twin = (t, y * 2 + (1 - h), c)
    at_core = (t, r, x * 2 + (1 - k))

    t0, t1 = rem(t, 2), lax.div(t, 2)
    tok_of = [rem(t0 + n % 2, 2) + 2 * rem(t1 + n // 2, 2) for n in range(4)]
    base_of = [[pl.multiple_of(b * 256 + u * T, T) for u in range(2)] for b in tok_of]

    mine = pl.ds(pl.multiple_of(t * 256, 256), 256)
    loads = [
        pltpu.make_async_copy(src, dst, ld_sem.at[n])
        for n, (src, dst) in enumerate(
            (
                (tokens, tc.at[0, mine]), (cot, tc.at[1, mine]),
                (gate_k, gk), (gate_w, gr), (up_k, uk), (up_w, ur),
                (down_k, dk), (down_w, dr_w),
            )
        )
    ]
    for copy in loads:
        copy.start()

    barrier = pltpu.get_barrier_semaphore()
    peers = [at_next, at_prev, at_twin]
    peers += [(t, r, col_of[n]) for n in range(1, 8)]
    peers += [(tok_of[n], r, c) for n in range(1, 4)]
    for peer in peers:
        pl.semaphore_signal(barrier, inc=1, device_id=peer, device_id_type=MESH)

    SEND = dict(az=0, ax=1, ac=2, rs=3, ag=4, d=5, z=6, o=7, dk=8, dl=9, zl=10, t=11)

    def send(src, dst, cls, recv, peer):
        pltpu.make_async_remote_copy(
            src_ref=src, dst_ref=dst, send_sem=send_sem.at[SEND[cls]], recv_sem=recv,
            device_id=peer, device_id_type=MESH,
        ).start()

    def wait(ref, sem):
        pltpu.make_async_copy(ref, ref, sem).wait()

    def base(i):
        return base_of[BLOCK[i]][HALF[i]]

    def rows(i, q, n=H):
        return pl.ds(pl.multiple_of(base(i) + q * n, n), n)

    def stage_az(i):
        for n in (0, 2) if BLOCK[i] == 1 else (0,):
            start = base_of[0][HALF[i]] + x_of[n] * 32
            at = pl.ds(pl.multiple_of(start, 32), 32)
            send(tc.at[k, at], tc.at[k, at], "az", az.at[i], (tok_of[BLOCK[i]], r, c))

    def stage_ax(i):
        near = BLOCK[i] == 1
        at = rows(i, x, 32)
        wait(tc.at[k, pl.ds(0, 64 if near else 32)], az.at[i])
        for n in (1, 3) if near else (1, 3, 2):
            send(tc.at[k, at], tc.at[k, at], "ax", ax.at[i], (t, r, x_col[n]))

    def stage_ac(i):
        wait(tc.at[k, pl.ds(0, 64 if BLOCK[i] == 1 else 96)], ax.at[i])
        at = rows(i, 0, T)
        send(tc.at[k, at], tc.at[k, at], "ac", ac.at[i], at_core)

    def forward(i, n):
        at = rows(i, 0, T)
        if n == 2:
            part = lax.dot_general(
                tc[1, at, :], dw[...], (((1,), (1,)), ((), ())), preferred_element_type=F32
            )
        else:
            part = jnp.dot(tc[0, at, :], (gw, uw)[n][...], preferred_element_type=F32)
        pre32[at, pl.ds(n * 512, 512)] = part
        pre[at, pl.ds(n * 512, 512)] = part.astype(BF)

    def stage_s1(i):
        if BLOCK[i]:
            wait(tc.at[1 - k, rows(i, 0, T)], ac.at[i])
        if i:
            for n in range(3):
                forward(i, n)
        send(pre.at[rows(i, y_opp * 2)], rx1.at[i, 0], "rs", s1.at[i], at_next)
        send(pre.at[rows(i, y_opp * 2 + 1)], rx1.at[i, 1], "rs", s1.at[i], at_prev)
        send(pre.at[rows(i, y_next * 2 + 1)], rx3.at[i, 0], "rs", s3.at[i], at_next)
        send(pre.at[rows(i, y_prev * 2)], rx3.at[i, 1], "rs", s3.at[i], at_prev)

    def stage_s2(i):
        wait(rx1.at[i], s1.at[i])
        acc[i, 0] = (rx1[i, 0].astype(F32) + pre32[rows(i, y_next * 2), :]).astype(BF)
        send(acc.at[i, 0], rx3.at[i, 2], "rs", s3.at[i], at_next)
        acc[i, 1] = (rx1[i, 1].astype(F32) + pre32[rows(i, y_prev * 2 + 1), :]).astype(BF)
        send(acc.at[i, 1], rx3.at[i, 3], "rs", s3.at[i], at_prev)

    def stage_s3(i):
        wait(rx3.at[i], s3.at[i])

        def total(half):
            return (
                pre32[rows(i, y * 2 + half), :]
                + rx3[i, 1 - half].astype(F32)
                + rx3[i, 2 + half].astype(F32)
            )

        if i in WHOLE:
            for half in range(2):
                part = total(half)
                hs[i, pl.ds(half * H, H)] = part.astype(BF)
                keep[i, pl.ds(half * H, H)] = part
            send(hs.at[i], hr.at[i], "rs", hrs.at[i], at_twin)
        else:
            first = pl.ds(0, H)
            hs[i, first] = total(1 - h).astype(BF)
            send(hs.at[i, first], hr.at[i, first], "rs", hrs.at[i], at_twin)
            keep[i, first] = total(h)

    def own_rows(i):
        return rows(i, y, 2 * H) if i in WHOLE else rows(i, r)

    def stage_s4(i):
        got = pl.ds(0, 2 * H if i in WHOLE else H)
        wait(hr.at[i, got], hrs.at[i])
        sums = keep[i, got] + hr[i, got].astype(F32)
        gate, up, back = sums[:, :512], sums[:, 512:1024], sums[:, 1024:]
        sig = jax.nn.sigmoid(gate)
        silu = gate * sig
        at = own_rows(i)
        hid[at, :] = (silu * up).astype(BF)
        act[at, pl.ds(0, 512)] = (back * up * (sig * (1.0 + gate * (1.0 - sig)))).astype(BF)
        act[at, pl.ds(512, 512)] = (back * silu).astype(BF)
        gather_own(i, act, "ag", gh, gy)

    def gather_own(i, ref, cls, twin_sem, ring_sem):
        at = own_rows(i)
        if i in WHOLE:
            send(ref.at[at], ref.at[at], cls, ring_sem.at[i, 0], at_next)
            send(ref.at[at], ref.at[at], cls, ring_sem.at[i, 0], at_prev)
            return
        send(ref.at[at], ref.at[at], cls, twin_sem.at[i], at_twin)
        send(ref.at[at], ref.at[at], cls, ring_sem.at[i, h], at_next)
        send(ref.at[at], ref.at[at], cls, ring_sem.at[i, 1 - h], at_prev)

    def gather_twin(i, ref, cls, twin_sem, ring_sem):
        at = rows(i, y * 2 + (1 - h))
        wait(ref.at[at], twin_sem.at[i])
        send(ref.at[at], ref.at[at], cls, ring_sem.at[i, 1 - h], at_next)
        send(ref.at[at], ref.at[at], cls, ring_sem.at[i, h], at_prev)

    def gather_far(i, ref, cls, ring_sem):
        wait(ref.at[pl.ds(0, (4 if i in WHOLE else 2) * H)], ring_sem.at[i, 0])
        at = rows(i, y_prev * 2)
        send(ref.at[at], ref.at[at], cls, ring_sem.at[i, 1], at_next)
        at = rows(i, y_next * 2 + 1)
        send(ref.at[at], ref.at[at], cls, ring_sem.at[i, 1], at_prev)

    def stage_s5(i):
        gather_twin(i, act, "ag", gh, gy)

    def stage_s6(i):
        gather_far(i, act, "ag", gy)

    def stage_t4(i):
        gather_own(i, hid, "t", th, ty)

    def stage_t5(i):
        gather_twin(i, hid, "t", th, ty)

    def stage_t6(i):
        gather_far(i, hid, "t", ty)

    def stage_t7(i):
        wait(hid.at[pl.ds(0, (2 if i in WHOLE else 4) * H)], ty.at[i, 1])

    def stage_s7(i):
        wait(act.at[pl.ds(0, (2 if i in WHOLE else 4) * H)], gy.at[i, 1])
        at = rows(i, 0, T)
        nt = (((1,), (1,)), ((), ()))
        part = lax.dot_general(
            act[at, pl.ds(0, 512)], gw[...], nt, preferred_element_type=F32
        ) + lax.dot_general(
            act[at, pl.ds(512, 512)], uw[...], nt, preferred_element_type=F32
        )
        d32[i] = part
        other = pl.ds(pl.multiple_of((1 - k) * 64, 64), 64)
        send(d32.at[i, other], dk32.at[i], "dk", dks.at[i], at_core)

    def stage_s7b(i):
        wait(dk32.at[i], dks.at[i])
        own = pl.ds(pl.multiple_of(k * 64, 64), 64)
        part = d32[i, own, :] + dk32[i]
        dk32[i] = part
        if i in NARROW:
            dpart[i] = part.astype(BF)
        for n in (1, 3, 2):
            at = pl.ds(pl.multiple_of(x_of[n] * H, H), H)
            to = (t, r, x_col[n])
            if i in NARROW:
                send(dpart.at[i, at], dr16.at[i, n - 1], "dl", drs.at[i], to)
            else:
                send(dk32.at[i, at], dr.at[i, n - 1], "d", drs.at[i], to)

    def stage_s8(i):
        came = dr16.at[i] if i in NARROW else dr.at[i]
        wait(came, drs.at[i])
        total = dk32[i, pl.ds(pl.multiple_of(x * H, H), H), :]
        for n in range(3):
            total = total + came[n].astype(F32)
        b, u = BLOCK[i], HALF[i]
        if b == 0:
            zown[u] = total
        elif i in NARROW:
            zs32[u, b] = total
            send(zs32.at[u, b], zr32.at[u, b], "zl", zrs.at[u, b], (tok_of[b], r, c))
        else:
            zs[u, b] = total.astype(BF)
            send(zs.at[u, b], zr.at[u, b], "z", zrs.at[u, b], (tok_of[b], r, c))

    def stage_s9(u):
        total = zown[u]
        for b in range(1, 4):
            narrow = any((BLOCK[i], HALF[i]) == (b, u) for i in NARROW)
            came = (zr32 if narrow else zr).at[u, b]
            wait(came, zrs.at[u, b])
            total = total + came[...].astype(F32)
        at = pl.ds(pl.multiple_of(u * T + (k * 4 + x) * H, H), H)
        obuf[at, :] = total.astype(BF)
        for n in range(7):
            send(obuf.at[at], obuf.at[at], "o", ors.at[u], (t, r, col_of[n + 1]))

    tn = (((0,), (0,)), ((), ()))

    def stage_g(n):
        if n == 2:
            tall[...] = lax.dot_general(
                hid[...], tc[1], tn, preferred_element_type=F32
            )
            finish(tall, dr_w, dk, down_g, down_s)
            return
        full[...] = lax.dot_general(
            tc[0], act[:, pl.ds(512 * n, 512)], tn, preferred_element_type=F32
        )
        if n == 0:
            finish(full, gr, gk, gate_g, gate_s)
        else:
            finish(full, ur, uk, up_g, up_s)

    def prepare(n):
        loads[2 + 2 * n].wait()
        loads[3 + 2 * n].wait()
        apply_mask((gr, ur, dr_w)[n], (gk, uk, dk)[n], (gw, uw, dw)[n])
        forward(0, n)

    loads[0].wait()
    loads[1].wait()
    prepare(0)
    pl.semaphore_wait(barrier, len(peers))
    for i in range(NCH):
        if BLOCK[i]:
            stage_az(i)
    prepare(1)
    prepare(2)
    stages = dict(
        ax=stage_ax, ac=stage_ac, s1=stage_s1, s2=stage_s2, s3=stage_s3, s4=stage_s4,
        s5=stage_s5, s6=stage_s6, s7=stage_s7, s7b=stage_s7b, s8=stage_s8, t4=stage_t4,
        t5=stage_t5, t6=stage_t6, t7=stage_t7, s9=stage_s9, g=stage_g,
    )
    for name, i in ORDER:
        stages[name](i)
    for u in range(2):
        wait(obuf.at[pl.ds(0, 7 * H)], ors.at[u])
    wait(tc.at[0, pl.ds(0, 8 * 32)], send_sem.at[0])
    wait(tc.at[0, pl.ds(0, 16 * 32)], send_sem.at[1])
    wait(tc.at[0, pl.ds(0, 6 * T)], send_sem.at[2])
    whole, narrow = len(WHOLE), len(NARROW)
    wait(pre.at[pl.ds(0, (56 + whole) * H)], send_sem.at[3])
    wait(act.at[pl.ds(0, (56 - whole) * H)], send_sem.at[4])
    wait(dr.at[pl.ds(0, NCH - narrow)], send_sem.at[5])
    far = sum(1 for i in range(NCH) if BLOCK[i] and i not in NARROW)
    wait(obuf.at[pl.ds(0, far * H)], send_sem.at[6])
    wait(obuf.at[pl.ds(0, 14 * H)], send_sem.at[7])
    wait(dk32, send_sem.at[8])
    wait(dr16.at[pl.ds(0, narrow)], send_sem.at[9])
    if far < 6:
        wait(dk32.at[0, pl.ds(0, (6 - far) * H)], send_sem.at[10])
    wait(hid.at[pl.ds(0, (56 - whole) * H)], send_sem.at[11])


def store_kernel(*refs):
    n = len(refs) // 2
    sems = refs[-1]
    copies = [
        pltpu.make_async_copy(refs[i], refs[n + i], sems.at[i]) for i in range(n)
    ]
    for copy in copies:
        copy.start()
    for copy in copies:
        copy.wait()


def on_device(*args):
    hbm = pl.BlockSpec(memory_space=pltpu.HBM)
    vmem = pl.BlockSpec(memory_space=pltpu.VMEM)
    dma = pltpu.SemaphoreType.DMA
    shapes = ((256, 1024),) + ((1024, 512), (1024, 512), (512, 1024)) * 2
    args = [pltpu.with_memory_space_constraint(a, pltpu.HBM) for a in args]
    outs = pl.pallas_call(
        comm_kernel,
        name="exchange",
        out_shape=[pltpu.VMEM(s, BF) for s in shapes],
        in_specs=[hbm] * 8,
        out_specs=[vmem] * 7,
        scratch_shapes=[
            pltpu.VMEM((2, 1024, 1024), BF),
            pltpu.VMEM((1024, 512), BF),
            pltpu.VMEM((1024, 512), BF),
            pltpu.VMEM((512, 1024), BF),
            pltpu.VMEM((1024, 512), BF),
            pltpu.VMEM((1024, 512), BF),
            pltpu.VMEM((512, 1024), BF),
            pltpu.VMEM((64, 512), jnp.int32),
            pltpu.VMEM((64, 512), jnp.int32),
            pltpu.VMEM((32, 1024), jnp.int32),
            pltpu.VMEM((1024, 1536), BF),
            pltpu.VMEM((1024, 1536), F32),
            pltpu.VMEM((NCH, 2, H, 1536), BF),
            pltpu.VMEM((NCH, 2, H, 1536), BF),
            pltpu.VMEM((NCH, 4, H, 1536), BF),
            pltpu.VMEM((NCH, 2 * H, 1536), BF),
            pltpu.VMEM((NCH, 2 * H, 1536), BF),
            pltpu.VMEM((NCH, 2 * H, 1536), F32),
            pltpu.VMEM((1024, 1024), BF),
            pltpu.VMEM((1024, 512), BF),
            pltpu.VMEM((NCH, 64, 1024), BF),
            pltpu.VMEM((NCH, T, 1024), F32),
            pltpu.VMEM((NCH, 64, 1024), F32),
            pltpu.VMEM((NCH, 3, H, 1024), F32),
            pltpu.VMEM((NCH, 3, H, 1024), BF),
            pltpu.VMEM((2, H, 1024), F32),
            pltpu.VMEM((2, 4, H, 1024), BF),
            pltpu.VMEM((2, 4, H, 1024), BF),
            pltpu.VMEM((2, 4, H, 1024), F32),
            pltpu.VMEM((2, 4, H, 1024), F32),
            pltpu.VMEM((1024, 512), F32),
            pltpu.VMEM((512, 1024), F32),
            dma((8,)),
            dma((12,)),
            dma((NCH,)),
            dma((NCH,)),
            dma((NCH,)),
            dma((NCH,)),
            dma((NCH,)),
            dma((NCH,)),
            dma((NCH,)),
            dma((NCH, 2)),
            dma((NCH,)),
            dma((NCH, 2)),
            dma((NCH,)),
            dma((NCH,)),
            dma((2, 4)),
            dma((2,)),
        ],
        compiler_params=pltpu.CompilerParams(
            collective_id=0, has_side_effects=True, vmem_limit_bytes=50 * 2**20
        ),
    )(*args)
    return tuple(
        pl.pallas_call(
            store_kernel,
            name="store",
            out_shape=[jax.ShapeDtypeStruct(s, BF) for s in shapes],
            in_specs=[vmem] * 7,
            out_specs=[hbm] * 7,
            scratch_shapes=[dma((7,))],
            compiler_params=pltpu.CompilerParams(vmem_limit_bytes=2**20),
        )(*[pltpu.with_memory_space_constraint(o, pltpu.VMEM) for o in outs])
    )


def solution(mesh):
    return jax.shard_map(
        on_device,
        mesh=mesh,
        in_specs=(
            P("tok", "row"),
            P("tok", "row"),
            P("row", ("tok", "col")),
            P("row", ("tok", "col")),
            P(("tok", "col"), "row"),
            P("row", ("tok", "col")),
            P("row", ("tok", "col")),
            P(("tok", "col"), "row"),
        ),
        out_specs=(
            P("tok", "row"),
            P("row", ("tok", "col")),
            P("row", ("tok", "col")),
            P(("tok", "col"), "row"),
            P("row", ("tok", "col")),
            P("row", ("tok", "col")),
            P(("tok", "col"), "row"),
        ),
        check_vma=False,
    )
```

```python
import functools

import jax
import jax.numpy as jnp
from jax import lax
from jax.experimental import pallas as pl
from jax.experimental.pallas import tpu as pltpu
from jax.sharding import PartitionSpec as P

MESH = pl.DeviceIdType.MESH
BF = jnp.bfloat16
F32 = jnp.float32
NCH = 8
T = 128
H = 16
BLOCK = (0, 0, 1, 2, 3, 3, 2, 1)
HALF = (0, 1, 0, 0, 0, 1, 1, 1)
WHOLE = (7,)
NARROW = (0, 1, 7,)
ORDER = (
    ("s1", 0), ("ax", 2), ("s2", 0), ("az", 5), ("s1", 1), ("az", 7), ("ax", 3), ("ac", 2), ("ax", 4),
    ("s3", 0), ("az", 6), ("s1", 2), ("s2", 1), ("ac", 3), ("ax", 5), ("s2", 2), ("s1", 3), ("ac", 4),
    ("s4", 0), ("ax", 6), ("s3", 1), ("s1", 4), ("ac", 5), ("s3", 2), ("s2", 3), ("s1", 5), ("ax", 7),
    ("s2", 4), ("ac", 6), ("s5", 0), ("s3", 3), ("s1", 6), ("ac", 7), ("s2", 5), ("s4", 2), ("s3", 4),
    ("s2", 6), ("s4", 3), ("s3", 5), ("s6", 0), ("s5", 2), ("s1", 7), ("s3", 6), ("s4", 4), ("s5", 3),
    ("s7", 0), ("s2", 7), ("s6", 2), ("s4", 5), ("s6", 3), ("s4", 6), ("s3", 7), ("s7b", 0), ("s5", 4),
    ("s7", 2), ("s5", 5), ("s7", 3), ("s7b", 2), ("s6", 4), ("s5", 6), ("t4", 0), ("s7b", 3), ("s4", 1),
    ("t4", 4), ("s6", 5), ("t4", 2), ("s7", 4), ("s6", 6), ("t4", 5), ("s4", 7), ("s8", 0), ("s7b", 4),
    ("s7", 5), ("s5", 1), ("s7", 6), ("s7b", 5), ("s6", 7), ("t4", 6), ("s8", 2), ("s8", 3), ("s7b", 6),
    ("s6", 1), ("t4", 1), ("t4", 3), ("t5", 4), ("t5", 0), ("s7", 7), ("s8", 4), ("s7", 1), ("s7b", 7),
    ("t5", 5), ("t4", 7), ("s8", 5), ("t5", 6), ("t6", 0), ("s7b", 1), ("t5", 2), ("t5", 1), ("t5", 3),
    ("t6", 4), ("s8", 6), ("t6", 5), ("s9", 0), ("s8", 7), ("t6", 6), ("t6", 2), ("g", 1), ("t6", 3),
    ("t6", 1), ("s8", 1), ("t7", 2), ("s9", 1), ("t6", 7), ("t7", 5), ("t7", 3), ("g", 0), ("t7", 6),
    ("t7", 1), ("t7", 4), ("t7", 0), ("t7", 7), ("g", 2),
)


def unpack(keep_ref, i, shifts):
    row = jnp.broadcast_to(keep_ref[pl.ds(i, 1), :], shifts.shape)
    return (jnp.right_shift(row, shifts) & 1).astype(F32)


def for_row_groups(keep_ref, body):
    shifts = lax.broadcasted_iota(jnp.int32, (16, keep_ref.shape[1]), 0)

    def one(i, _):
        body(pl.ds(pl.multiple_of(i * 16, 16), 16), unpack(keep_ref, i, shifts))
        return 0

    lax.fori_loop(0, keep_ref.shape[0], one, 0, unroll=4)


def apply_mask(w_ref, keep_ref, eff_ref):
    def body(at, bits):
        eff_ref[at, :] = (w_ref[at, :].astype(F32) * bits).astype(BF)

    for_row_groups(keep_ref, body)


def finish(full_ref, w_ref, keep_ref, grad_ref, score_ref):
    def body(at, bits):
        full = full_ref[at, :]
        grad_ref[at, :] = (full * bits).astype(BF)
        score_ref[at, :] = (-(w_ref[at, :].astype(F32) * full)).astype(BF)

    for_row_groups(keep_ref, body)


def comm_kernel(
    tokens, cot, gate_w, up_w, down_w, gate_k, up_k, down_k,
    obuf, gate_g, up_g, down_g, gate_s, up_s, down_s,
    tc, gr, ur, dr_w, gw, uw, dw, gk, uk, dk, pre, pre32, rx1, acc, rx3, hs, hr, keep, act, hid,
    dpart, d32, dk32, dr, dr16, zown, zs, zr, zs32, zr32, full, tall,
    ld_sem, send_sem, az, ax, ac, s1, s3, hrs, gh, gy, th, ty, dks, drs, zrs, ors,
):
    t = lax.axis_index("tok")
    r = lax.axis_index("row")
    c = lax.axis_index("col")
    rem = lax.rem
    h, k = rem(r, 2), rem(c, 2)
    y, x = lax.div(r, 2), lax.div(c, 2)
    y_next, y_prev, y_opp = rem(y + 1, 4), rem(y + 3, 4), rem(y + 2, 4)
    x_of = [rem(x + n, 4) for n in range(4)]
    x_col = [at_x * 2 + k for at_x in x_of]
    col_of = [rem(c + n, 8) for n in range(8)]
    at_next, at_prev = (t, y_next * 2 + h, c), (t, y_prev * 2 + h, c)
    at_twin = (t, y * 2 + (1 - h), c)
    at_core = (t, r, x * 2 + (1 - k))

    t0, t1 = rem(t, 2), lax.div(t, 2)
    tok_of = [rem(t0 + n % 2, 2) + 2 * rem(t1 + n // 2, 2) for n in range(4)]
    base_of = [[pl.multiple_of(b * 256 + u * T, T) for u in range(2)] for b in tok_of]

    barrier = pltpu.get_barrier_semaphore()
    peers = [at_next, at_prev, at_twin]
    peers += [(t, r, col_of[n]) for n in range(1, 8)]
    peers += [(tok_of[n], r, c) for n in range(1, 4)]
    for peer in peers:
        pl.semaphore_signal(barrier, inc=1, device_id=peer, device_id_type=MESH)

    mine = pl.ds(pl.multiple_of(t * 256, 256), 256)
    loads = [
        pltpu.make_async_copy(src, dst, ld_sem.at[n])
        for n, (src, dst) in enumerate(
            (
                (tokens, tc.at[0, mine]), (cot, tc.at[1, mine]),
                (gate_k, gk), (gate_w, gr), (up_k, uk), (up_w, ur),
                (down_k, dk), (down_w, dr_w),
            )
        )
    ]
    for copy in loads:
        copy.start()

    SEND = dict(az=0, ax=1, ac=2, rs=3, ag=4, d=5, z=6, o=7, dk=8, dl=9, zl=10, t=11)

    def send(src, dst, cls, recv, peer):
        pltpu.make_async_remote_copy(
            src_ref=src, dst_ref=dst, send_sem=send_sem.at[SEND[cls]], recv_sem=recv,
            device_id=peer, device_id_type=MESH,
        ).start()

    def wait(ref, sem):
        pltpu.make_async_copy(ref, ref, sem).wait()

    def base(i):
        return base_of[BLOCK[i]][HALF[i]]

    def rows(i, q, n=H):
        return pl.ds(pl.multiple_of(base(i) + q * n, n), n)

    def stage_az(i):
        for n in (0, 2) if BLOCK[i] == 1 else (0,):
            start = base_of[0][HALF[i]] + x_of[n] * 32
            at = pl.ds(pl.multiple_of(start, 32), 32)
            send(tc.at[k, at], tc.at[k, at], "az", az.at[i], (tok_of[BLOCK[i]], r, c))

    def stage_ax(i):
        near = BLOCK[i] == 1
        at = rows(i, x, 32)
        wait(tc.at[k, pl.ds(0, 64 if near else 32)], az.at[i])
        for n in (1, 3) if near else (1, 3, 2):
            send(tc.at[k, at], tc.at[k, at], "ax", ax.at[i], (t, r, x_col[n]))

    def stage_ac(i):
        wait(tc.at[k, pl.ds(0, 64 if BLOCK[i] == 1 else 96)], ax.at[i])
        at = rows(i, 0, T)
        send(tc.at[k, at], tc.at[k, at], "ac", ac.at[i], at_core)

    def forward(i, n):
        at = rows(i, 0, T)
        if n == 2:
            part = lax.dot_general(
                tc[1, at, :], dw[...], (((1,), (1,)), ((), ())), preferred_element_type=F32
            )
        else:
            part = jnp.dot(tc[0, at, :], (gw, uw)[n][...], preferred_element_type=F32)
        pre32[at, pl.ds(n * 512, 512)] = part
        pre[at, pl.ds(n * 512, 512)] = part.astype(BF)

    def stage_s1(i):
        if BLOCK[i]:
            wait(tc.at[1 - k, rows(i, 0, T)], ac.at[i])
        if i:
            for n in range(3):
                forward(i, n)
        send(pre.at[rows(i, y_opp * 2)], rx1.at[i, 0], "rs", s1.at[i], at_next)
        send(pre.at[rows(i, y_opp * 2 + 1)], rx1.at[i, 1], "rs", s1.at[i], at_prev)
        send(pre.at[rows(i, y_next * 2 + 1)], rx3.at[i, 0], "rs", s3.at[i], at_next)
        send(pre.at[rows(i, y_prev * 2)], rx3.at[i, 1], "rs", s3.at[i], at_prev)

    def stage_s2(i):
        wait(rx1.at[i], s1.at[i])
        acc[i, 0] = (rx1[i, 0].astype(F32) + pre32[rows(i, y_next * 2), :]).astype(BF)
        send(acc.at[i, 0], rx3.at[i, 2], "rs", s3.at[i], at_next)
        acc[i, 1] = (rx1[i, 1].astype(F32) + pre32[rows(i, y_prev * 2 + 1), :]).astype(BF)
        send(acc.at[i, 1], rx3.at[i, 3], "rs", s3.at[i], at_prev)

    def stage_s3(i):
        wait(rx3.at[i], s3.at[i])

        def total(half):
            return (
                pre32[rows(i, y * 2 + half), :]
                + rx3[i, 1 - half].astype(F32)
                + rx3[i, 2 + half].astype(F32)
            )

        if i in WHOLE:
            for half in range(2):
                part = total(half)
                hs[i, pl.ds(half * H, H)] = part.astype(BF)
                keep[i, pl.ds(half * H, H)] = part
            send(hs.at[i], hr.at[i], "rs", hrs.at[i], at_twin)
        else:
            first = pl.ds(0, H)
            hs[i, first] = total(1 - h).astype(BF)
            send(hs.at[i, first], hr.at[i, first], "rs", hrs.at[i], at_twin)
            keep[i, first] = total(h)

    def own_rows(i):
        return rows(i, y, 2 * H) if i in WHOLE else rows(i, r)

    def stage_s4(i):
        got = pl.ds(0, 2 * H if i in WHOLE else H)
        wait(hr.at[i, got], hrs.at[i])
        sums = keep[i, got] + hr[i, got].astype(F32)
        gate, up, back = sums[:, :512], sums[:, 512:1024], sums[:, 1024:]
        sig = jax.nn.sigmoid(gate)
        silu = gate * sig
        at = own_rows(i)
        hid[at, :] = (silu * up).astype(BF)
        act[at, pl.ds(0, 512)] = (back * up * (sig * (1.0 + gate * (1.0 - sig)))).astype(BF)
        act[at, pl.ds(512, 512)] = (back * silu).astype(BF)
        gather_own(i, act, "ag", gh, gy)

    def gather_own(i, ref, cls, twin_sem, ring_sem):
        at = own_rows(i)
        if i in WHOLE:
            send(ref.at[at], ref.at[at], cls, ring_sem.at[i, 0], at_next)
            send(ref.at[at], ref.at[at], cls, ring_sem.at[i, 0], at_prev)
            return
        send(ref.at[at], ref.at[at], cls, twin_sem.at[i], at_twin)
        send(ref.at[at], ref.at[at], cls, ring_sem.at[i, h], at_next)
        send(ref.at[at], ref.at[at], cls, ring_sem.at[i, 1 - h], at_prev)

    def gather_twin(i, ref, cls, twin_sem, ring_sem):
        at = rows(i, y * 2 + (1 - h))
        wait(ref.at[at], twin_sem.at[i])
        send(ref.at[at], ref.at[at], cls, ring_sem.at[i, 1 - h], at_next)
        send(ref.at[at], ref.at[at], cls, ring_sem.at[i, h], at_prev)

    def gather_far(i, ref, cls, ring_sem):
        wait(ref.at[pl.ds(0, (4 if i in WHOLE else 2) * H)], ring_sem.at[i, 0])
        at = rows(i, y_prev * 2)
        send(ref.at[at], ref.at[at], cls, ring_sem.at[i, 1], at_next)
        at = rows(i, y_next * 2 + 1)
        send(ref.at[at], ref.at[at], cls, ring_sem.at[i, 1], at_prev)

    def stage_s5(i):
        gather_twin(i, act, "ag", gh, gy)

    def stage_s6(i):
        gather_far(i, act, "ag", gy)

    def stage_t4(i):
        gather_own(i, hid, "t", th, ty)

    def stage_t5(i):
        gather_twin(i, hid, "t", th, ty)

    def stage_t6(i):
        gather_far(i, hid, "t", ty)

    def stage_t7(i):
        wait(hid.at[pl.ds(0, (2 if i in WHOLE else 4) * H)], ty.at[i, 1])

    def stage_s7(i):
        wait(act.at[pl.ds(0, (2 if i in WHOLE else 4) * H)], gy.at[i, 1])
        at = rows(i, 0, T)
        nt = (((1,), (1,)), ((), ()))
        part = lax.dot_general(
            act[at, pl.ds(0, 512)], gw[...], nt, preferred_element_type=F32
        ) + lax.dot_general(
            act[at, pl.ds(512, 512)], uw[...], nt, preferred_element_type=F32
        )
        d32[i] = part
        other = pl.ds(pl.multiple_of((1 - k) * 64, 64), 64)
        send(d32.at[i, other], dk32.at[i], "dk", dks.at[i], at_core)

    def stage_s7b(i):
        wait(dk32.at[i], dks.at[i])
        own = pl.ds(pl.multiple_of(k * 64, 64), 64)
        part = d32[i, own, :] + dk32[i]
        dk32[i] = part
        if i in NARROW:
            dpart[i] = part.astype(BF)
        for n in (1, 3, 2):
            at = pl.ds(pl.multiple_of(x_of[n] * H, H), H)
            to = (t, r, x_col[n])
            if i in NARROW:
                send(dpart.at[i, at], dr16.at[i, n - 1], "dl", drs.at[i], to)
            else:
                send(dk32.at[i, at], dr.at[i, n - 1], "d", drs.at[i], to)

    def stage_s8(i):
        came = dr16.at[i] if i in NARROW else dr.at[i]
        wait(came, drs.at[i])
        total = dk32[i, pl.ds(pl.multiple_of(x * H, H), H), :]
        for n in range(3):
            total = total + came[n].astype(F32)
        b, u = BLOCK[i], HALF[i]
        if b == 0:
            zown[u] = total
        elif i in NARROW:
            zs32[u, b] = total
            send(zs32.at[u, b], zr32.at[u, b], "zl", zrs.at[u, b], (tok_of[b], r, c))
        else:
            zs[u, b] = total.astype(BF)
            send(zs.at[u, b], zr.at[u, b], "z", zrs.at[u, b], (tok_of[b], r, c))

    def stage_s9(u):
        total = zown[u]
        for b in range(1, 4):
            narrow = any((BLOCK[i], HALF[i]) == (b, u) for i in NARROW)
            came = (zr32 if narrow else zr).at[u, b]
            wait(came, zrs.at[u, b])
            total = total + came[...].astype(F32)
        at = pl.ds(pl.multiple_of(u * T + (k * 4 + x) * H, H), H)
        obuf[at, :] = total.astype(BF)
        for n in range(7):
            send(obuf.at[at], obuf.at[at], "o", ors.at[u], (t, r, col_of[n + 1]))

    tn = (((0,), (0,)), ((), ()))

    def stage_g(n):
        if n == 2:
            tall[...] = lax.dot_general(
                hid[...], tc[1], tn, preferred_element_type=F32
            )
            finish(tall, dr_w, dk, down_g, down_s)
            return
        full[...] = lax.dot_general(
            tc[0], act[:, pl.ds(512 * n, 512)], tn, preferred_element_type=F32
        )
        if n == 0:
            finish(full, gr, gk, gate_g, gate_s)
        else:
            finish(full, ur, uk, up_g, up_s)

    def prepare(n):
        loads[2 + 2 * n].wait()
        loads[3 + 2 * n].wait()
        apply_mask((gr, ur, dr_w)[n], (gk, uk, dk)[n], (gw, uw, dw)[n])
        forward(0, n)

    loads[0].wait()
    loads[1].wait()
    prepare(0)
    pl.semaphore_wait(barrier, len(peers))
    for i in range(NCH):
        if BLOCK[i] and ("az", i) not in ORDER:
            stage_az(i)
    prepare(1)
    prepare(2)
    stages = dict(
        az=stage_az, ax=stage_ax, ac=stage_ac, s1=stage_s1, s2=stage_s2, s3=stage_s3, s4=stage_s4,
        s5=stage_s5, s6=stage_s6, s7=stage_s7, s7b=stage_s7b, s8=stage_s8, t4=stage_t4,
        t5=stage_t5, t6=stage_t6, t7=stage_t7, s9=stage_s9, g=stage_g,
    )
    for name, i in ORDER:
        stages[name](i)
    for u in range(2):
        wait(obuf.at[pl.ds(0, 7 * H)], ors.at[u])
    wait(tc.at[0, pl.ds(0, 8 * 32)], send_sem.at[0])
    wait(tc.at[0, pl.ds(0, 16 * 32)], send_sem.at[1])
    wait(tc.at[0, pl.ds(0, 6 * T)], send_sem.at[2])
    whole, narrow = len(WHOLE), len(NARROW)
    wait(pre.at[pl.ds(0, (56 + whole) * H)], send_sem.at[3])
    wait(act.at[pl.ds(0, (56 - whole) * H)], send_sem.at[4])
    wait(dr.at[pl.ds(0, NCH - narrow)], send_sem.at[5])
    far = sum(1 for i in range(NCH) if BLOCK[i] and i not in NARROW)
    wait(obuf.at[pl.ds(0, far * H)], send_sem.at[6])
    wait(obuf.at[pl.ds(0, 14 * H)], send_sem.at[7])
    wait(dk32, send_sem.at[8])
    wait(dr16.at[pl.ds(0, narrow)], send_sem.at[9])
    if far < 6:
        wait(dk32.at[0, pl.ds(0, (6 - far) * H)], send_sem.at[10])
    wait(hid.at[pl.ds(0, (56 - whole) * H)], send_sem.at[11])


def store_kernel(*refs):
    n = len(refs) // 2
    sems = refs[-1]
    copies = [
        pltpu.make_async_copy(refs[i], refs[n + i], sems.at[i]) for i in range(n)
    ]
    for copy in copies:
        copy.start()
    for copy in copies:
        copy.wait()


def on_device(*args):
    hbm = pl.BlockSpec(memory_space=pltpu.HBM)
    vmem = pl.BlockSpec(memory_space=pltpu.VMEM)
    dma = pltpu.SemaphoreType.DMA
    shapes = ((256, 1024),) + ((1024, 512), (1024, 512), (512, 1024)) * 2
    args = [pltpu.with_memory_space_constraint(a, pltpu.HBM) for a in args]
    outs = pl.pallas_call(
        comm_kernel,
        name="exchange",
        out_shape=[pltpu.VMEM(s, BF) for s in shapes],
        in_specs=[hbm] * 8,
        out_specs=[vmem] * 7,
        scratch_shapes=[
            pltpu.VMEM((2, 1024, 1024), BF),
            pltpu.VMEM((1024, 512), BF),
            pltpu.VMEM((1024, 512), BF),
            pltpu.VMEM((512, 1024), BF),
            pltpu.VMEM((1024, 512), BF),
            pltpu.VMEM((1024, 512), BF),
            pltpu.VMEM((512, 1024), BF),
            pltpu.VMEM((64, 512), jnp.int32),
            pltpu.VMEM((64, 512), jnp.int32),
            pltpu.VMEM((32, 1024), jnp.int32),
            pltpu.VMEM((1024, 1536), BF),
            pltpu.VMEM((1024, 1536), F32),
            pltpu.VMEM((NCH, 2, H, 1536), BF),
            pltpu.VMEM((NCH, 2, H, 1536), BF),
            pltpu.VMEM((NCH, 4, H, 1536), BF),
            pltpu.VMEM((NCH, 2 * H, 1536), BF),
            pltpu.VMEM((NCH, 2 * H, 1536), BF),
            pltpu.VMEM((NCH, 2 * H, 1536), F32),
            pltpu.VMEM((1024, 1024), BF),
            pltpu.VMEM((1024, 512), BF),
            pltpu.VMEM((NCH, 64, 1024), BF),
            pltpu.VMEM((NCH, T, 1024), F32),
            pltpu.VMEM((NCH, 64, 1024), F32),
            pltpu.VMEM((NCH, 3, H, 1024), F32),
            pltpu.VMEM((NCH, 3, H, 1024), BF),
            pltpu.VMEM((2, H, 1024), F32),
            pltpu.VMEM((2, 4, H, 1024), BF),
            pltpu.VMEM((2, 4, H, 1024), BF),
            pltpu.VMEM((2, 4, H, 1024), F32),
            pltpu.VMEM((2, 4, H, 1024), F32),
            pltpu.VMEM((1024, 512), F32),
            pltpu.VMEM((512, 1024), F32),
            dma((8,)),
            dma((12,)),
            dma((NCH,)),
            dma((NCH,)),
            dma((NCH,)),
            dma((NCH,)),
            dma((NCH,)),
            dma((NCH,)),
            dma((NCH,)),
            dma((NCH, 2)),
            dma((NCH,)),
            dma((NCH, 2)),
            dma((NCH,)),
            dma((NCH,)),
            dma((2, 4)),
            dma((2,)),
        ],
        compiler_params=pltpu.CompilerParams(
            collective_id=0, has_side_effects=True, vmem_limit_bytes=50 * 2**20
        ),
    )(*args)
    return tuple(
        pl.pallas_call(
            store_kernel,
            name="store",
            out_shape=[jax.ShapeDtypeStruct(s, BF) for s in shapes],
            in_specs=[vmem] * 7,
            out_specs=[hbm] * 7,
            scratch_shapes=[dma((7,))],
            compiler_params=pltpu.CompilerParams(vmem_limit_bytes=2**20),
        )(*[pltpu.with_memory_space_constraint(o, pltpu.VMEM) for o in outs])
    )


def solution(mesh):
    return jax.shard_map(
        on_device,
        mesh=mesh,
        in_specs=(
            P("tok", "row"),
            P("tok", "row"),
            P("row", ("tok", "col")),
            P("row", ("tok", "col")),
            P(("tok", "col"), "row"),
            P("row", ("tok", "col")),
            P("row", ("tok", "col")),
            P(("tok", "col"), "row"),
        ),
        out_specs=(
            P("tok", "row"),
            P("row", ("tok", "col")),
            P("row", ("tok", "col")),
            P(("tok", "col"), "row"),
            P("row", ("tok", "col")),
            P("row", ("tok", "col")),
            P(("tok", "col"), "row"),
        ),
        check_vma=False,
    )
```

```python
import functools

import jax
import jax.numpy as jnp
from jax import lax
from jax.experimental import pallas as pl
from jax.experimental.pallas import tpu as pltpu
from jax.sharding import PartitionSpec as P

MESH = pl.DeviceIdType.MESH
BF = jnp.bfloat16
F32 = jnp.float32
NCH = 8
T = 128
H = 16
BLOCK = (0, 0, 1, 2, 3, 3, 2, 1)
HALF = (0, 1, 0, 0, 0, 1, 1, 1)
WHOLE = (7,)
NARROW = (0, 1, 7,)
ORDER = (
    ("s1", 0), ("s2", 0), ("az", 5), ("az", 6), ("ax", 2), ("s1", 1), ("ax", 3), ("s3", 0), ("ac", 2),
    ("ax", 4), ("s2", 1), ("s1", 2), ("ac", 3), ("ax", 5), ("az", 7), ("s1", 3), ("s3", 1), ("ac", 4),
    ("s2", 2), ("ax", 6), ("s1", 4), ("s2", 3), ("ac", 5), ("s4", 0), ("s3", 2), ("ax", 7), ("s1", 5),
    ("ac", 6), ("s2", 4), ("s3", 3), ("s1", 6), ("s2", 5), ("s5", 0), ("s4", 2), ("s3", 4), ("s2", 6),
    ("s4", 3), ("ac", 7), ("s3", 5), ("s5", 2), ("s6", 0), ("s1", 7), ("s3", 6), ("s5", 3), ("s6", 2),
    ("s4", 4), ("s7", 0), ("s2", 7), ("s4", 5), ("s6", 3), ("s7b", 0), ("s4", 6), ("s7", 2), ("s5", 4),
    ("s3", 7), ("s4", 1), ("t4", 4), ("s5", 5), ("s7b", 2), ("s7", 3), ("s8", 0), ("s6", 4), ("s5", 6),
    ("t4", 2), ("t4", 6), ("s7b", 3), ("s6", 5), ("t4", 0), ("t4", 5), ("s7", 4), ("s6", 6), ("t4", 1),
    ("s8", 2), ("s4", 7), ("s7b", 4), ("s7", 5), ("s5", 1), ("s7", 6), ("s8", 3), ("s7b", 5), ("s6", 7),
    ("t4", 3), ("s7b", 6), ("s6", 1), ("t5", 5), ("t5", 6), ("t4", 7), ("t5", 0), ("t5", 2), ("t5", 1),
    ("s7", 7), ("s8", 4), ("s7", 1), ("s8", 5), ("s7b", 7), ("t6", 0), ("t5", 4), ("t5", 3), ("s7b", 1),
    ("t6", 7), ("t6", 5), ("t6", 2), ("s8", 6), ("s9", 0), ("s8", 7), ("t6", 6), ("g", 0), ("t6", 1),
    ("t6", 4), ("t7", 6), ("s8", 1), ("t6", 3), ("s9", 1), ("t7", 7), ("g", 1), ("t7", 3), ("t7", 0),
    ("t7", 4), ("t7", 2), ("t7", 5), ("t7", 1), ("g", 2),
)


def unpack(keep_ref, i, shifts):
    row = jnp.broadcast_to(keep_ref[pl.ds(i, 1), :], shifts.shape)
    return (jnp.right_shift(row, shifts) & 1).astype(F32)


def for_row_groups(keep_ref, body):
    shifts = lax.broadcasted_iota(jnp.int32, (16, keep_ref.shape[1]), 0)

    def one(i, _):
        body(pl.ds(pl.multiple_of(i * 16, 16), 16), unpack(keep_ref, i, shifts))
        return 0

    lax.fori_loop(0, keep_ref.shape[0], one, 0, unroll=4)


def apply_mask(w_ref, keep_ref, eff_ref):
    def body(at, bits):
        eff_ref[at, :] = (w_ref[at, :].astype(F32) * bits).astype(BF)

    for_row_groups(keep_ref, body)


def finish(full_ref, w_ref, keep_ref, grad_ref, score_ref):
    def body(at, bits):
        full = full_ref[at, :]
        grad_ref[at, :] = (full * bits).astype(BF)
        score_ref[at, :] = (-(w_ref[at, :].astype(F32) * full)).astype(BF)

    for_row_groups(keep_ref, body)


def comm_kernel(
    tokens, cot, gate_w, up_w, down_w, gate_k, up_k, down_k,
    obuf, gate_g, up_g, down_g, gate_s, up_s, down_s,
    tc, gr, ur, dr_w, gw, uw, dw, gk, uk, dk, pre, pre32, rx1, acc, rx3, hs, hr, keep, act, hid,
    dpart, d32, dk32, dr, dr16, zown, zs, zr, zs32, zr32, full, tall,
    ld_sem, send_sem, az, ax, ac, s1, s3, hrs, gh, gy, th, ty, dks, drs, zrs, ors,
):
    t = lax.axis_index("tok")
    r = lax.axis_index("row")
    c = lax.axis_index("col")
    rem = lax.rem
    h, k = rem(r, 2), rem(c, 2)
    y, x = lax.div(r, 2), lax.div(c, 2)
    y_next, y_prev, y_opp = rem(y + 1, 4), rem(y + 3, 4), rem(y + 2, 4)
    x_of = [rem(x + n, 4) for n in range(4)]
    x_col = [at_x * 2 + k for at_x in x_of]
    col_of = [rem(c + n, 8) for n in range(8)]
    at_next, at_prev = (t, y_next * 2 + h, c), (t, y_prev * 2 + h, c)
    at_twin = (t, y * 2 + (1 - h), c)
    at_core = (t, r, x * 2 + (1 - k))

    t0, t1 = rem(t, 2), lax.div(t, 2)
    tok_of = [rem(t0 + n % 2, 2) + 2 * rem(t1 + n // 2, 2) for n in range(4)]
    base_of = [[pl.multiple_of(b * 256 + u * T, T) for u in range(2)] for b in tok_of]

    barrier = pltpu.get_barrier_semaphore()
    peers = [at_next, at_prev, at_twin]
    peers += [(t, r, col_of[n]) for n in range(1, 8)]
    peers += [(tok_of[n], r, c) for n in range(1, 4)]
    for peer in peers:
        pl.semaphore_signal(barrier, inc=1, device_id=peer, device_id_type=MESH)

    mine = pl.ds(pl.multiple_of(t * 256, 256), 256)
    loads = [
        pltpu.make_async_copy(src, dst, ld_sem.at[n])
        for n, (src, dst) in enumerate(
            (
                (tokens, tc.at[0, mine]), (cot, tc.at[1, mine]),
                (gate_k, gk), (gate_w, gr), (up_k, uk), (up_w, ur),
                (down_k, dk), (down_w, dr_w),
            )
        )
    ]
    for copy in loads:
        copy.start()

    SEND = dict(az=0, ax=1, ac=2, rs=3, ag=4, d=5, z=6, o=7, dk=8, dl=9, zl=10, t=11)

    def send(src, dst, cls, recv, peer):
        pltpu.make_async_remote_copy(
            src_ref=src, dst_ref=dst, send_sem=send_sem.at[SEND[cls]], recv_sem=recv,
            device_id=peer, device_id_type=MESH,
        ).start()

    def wait(ref, sem):
        pltpu.make_async_copy(ref, ref, sem).wait()

    def base(i):
        return base_of[BLOCK[i]][HALF[i]]

    def rows(i, q, n=H):
        return pl.ds(pl.multiple_of(base(i) + q * n, n), n)

    def stage_az(i):
        for n in (0, 2) if BLOCK[i] == 1 else (0,):
            start = base_of[0][HALF[i]] + x_of[n] * 32
            at = pl.ds(pl.multiple_of(start, 32), 32)
            send(tc.at[k, at], tc.at[k, at], "az", az.at[i], (tok_of[BLOCK[i]], r, c))

    def stage_ax(i):
        near = BLOCK[i] == 1
        at = rows(i, x, 32)
        wait(tc.at[k, pl.ds(0, 64 if near else 32)], az.at[i])
        for n in (1, 3) if near else (2, 1, 3):
            send(tc.at[k, at], tc.at[k, at], "ax", ax.at[i], (t, r, x_col[n]))

    def stage_ac(i):
        wait(tc.at[k, pl.ds(0, 64 if BLOCK[i] == 1 else 96)], ax.at[i])
        at = rows(i, 0, T)
        send(tc.at[k, at], tc.at[k, at], "ac", ac.at[i], at_core)

    def forward(i, n):
        at = rows(i, 0, T)
        if n == 2:
            part = lax.dot_general(
                tc[1, at, :], dw[...], (((1,), (1,)), ((), ())), preferred_element_type=F32
            )
        else:
            part = jnp.dot(tc[0, at, :], (gw, uw)[n][...], preferred_element_type=F32)
        pre32[at, pl.ds(n * 512, 512)] = part
        pre[at, pl.ds(n * 512, 512)] = part.astype(BF)

    def stage_s1(i):
        if BLOCK[i]:
            wait(tc.at[1 - k, rows(i, 0, T)], ac.at[i])
        if i:
            for n in range(3):
                forward(i, n)
        send(pre.at[rows(i, y_opp * 2)], rx1.at[i, 0], "rs", s1.at[i], at_next)
        send(pre.at[rows(i, y_opp * 2 + 1)], rx1.at[i, 1], "rs", s1.at[i], at_prev)
        send(pre.at[rows(i, y_next * 2 + 1)], rx3.at[i, 0], "rs", s3.at[i], at_next)
        send(pre.at[rows(i, y_prev * 2)], rx3.at[i, 1], "rs", s3.at[i], at_prev)

    def stage_s2(i):
        wait(rx1.at[i], s1.at[i])
        acc[i, 0] = (rx1[i, 0].astype(F32) + pre32[rows(i, y_next * 2), :]).astype(BF)
        send(acc.at[i, 0], rx3.at[i, 2], "rs", s3.at[i], at_next)
        acc[i, 1] = (rx1[i, 1].astype(F32) + pre32[rows(i, y_prev * 2 + 1), :]).astype(BF)
        send(acc.at[i, 1], rx3.at[i, 3], "rs", s3.at[i], at_prev)

    def stage_s3(i):
        wait(rx3.at[i], s3.at[i])

        def total(half):
            return (
                pre32[rows(i, y * 2 + half), :]
                + rx3[i, 1 - half].astype(F32)
                + rx3[i, 2 + half].astype(F32)
            )

        if i in WHOLE:
            for half in range(2):
                part = total(half)
                hs[i, pl.ds(half * H, H)] = part.astype(BF)
                keep[i, pl.ds(half * H, H)] = part
            send(hs.at[i], hr.at[i], "rs", hrs.at[i], at_twin)
        else:
            first = pl.ds(0, H)
            hs[i, first] = total(1 - h).astype(BF)
            send(hs.at[i, first], hr.at[i, first], "rs", hrs.at[i], at_twin)
            keep[i, first] = total(h)

    def own_rows(i):
        return rows(i, y, 2 * H) if i in WHOLE else rows(i, r)

    def stage_s4(i):
        got = pl.ds(0, 2 * H if i in WHOLE else H)
        wait(hr.at[i, got], hrs.at[i])
        sums = keep[i, got] + hr[i, got].astype(F32)
        gate, up, back = sums[:, :512], sums[:, 512:1024], sums[:, 1024:]
        sig = jax.nn.sigmoid(gate)
        silu = gate * sig
        at = own_rows(i)
        hid[at, :] = (silu * up).astype(BF)
        act[at, pl.ds(0, 512)] = (back * up * (sig * (1.0 + gate * (1.0 - sig)))).astype(BF)
        act[at, pl.ds(512, 512)] = (back * silu).astype(BF)
        gather_own(i, act, "ag", gh, gy)

    def gather_own(i, ref, cls, twin_sem, ring_sem):
        at = own_rows(i)
        if i in WHOLE:
            send(ref.at[at], ref.at[at], cls, ring_sem.at[i, 0], at_next)
            send(ref.at[at], ref.at[at], cls, ring_sem.at[i, 0], at_prev)
            return
        send(ref.at[at], ref.at[at], cls, twin_sem.at[i], at_twin)
        send(ref.at[at], ref.at[at], cls, ring_sem.at[i, h], at_next)
        send(ref.at[at], ref.at[at], cls, ring_sem.at[i, 1 - h], at_prev)

    def gather_twin(i, ref, cls, twin_sem, ring_sem):
        at = rows(i, y * 2 + (1 - h))
        wait(ref.at[at], twin_sem.at[i])
        send(ref.at[at], ref.at[at], cls, ring_sem.at[i, 1 - h], at_next)
        send(ref.at[at], ref.at[at], cls, ring_sem.at[i, h], at_prev)

    def gather_far(i, ref, cls, ring_sem):
        wait(ref.at[pl.ds(0, (4 if i in WHOLE else 2) * H)], ring_sem.at[i, 0])
        at = rows(i, y_prev * 2)
        send(ref.at[at], ref.at[at], cls, ring_sem.at[i, 1], at_next)
        at = rows(i, y_next * 2 + 1)
        send(ref.at[at], ref.at[at], cls, ring_sem.at[i, 1], at_prev)

    def stage_s5(i):
        gather_twin(i, act, "ag", gh, gy)

    def stage_s6(i):
        gather_far(i, act, "ag", gy)

    def stage_t4(i):
        gather_own(i, hid, "t", th, ty)

    def stage_t5(i):
        gather_twin(i, hid, "t", th, ty)

    def stage_t6(i):
        gather_far(i, hid, "t", ty)

    def stage_t7(i):
        wait(hid.at[pl.ds(0, (2 if i in WHOLE else 4) * H)], ty.at[i, 1])

    def stage_s7(i):
        wait(act.at[pl.ds(0, (2 if i in WHOLE else 4) * H)], gy.at[i, 1])
        at = rows(i, 0, T)
        nt = (((1,), (1,)), ((), ()))
        part = lax.dot_general(
            act[at, pl.ds(0, 512)], gw[...], nt, preferred_element_type=F32
        ) + lax.dot_general(
            act[at, pl.ds(512, 512)], uw[...], nt, preferred_element_type=F32
        )
        d32[i] = part
        other = pl.ds(pl.multiple_of((1 - k) * 64, 64), 64)
        send(d32.at[i, other], dk32.at[i], "dk", dks.at[i], at_core)

    def stage_s7b(i):
        wait(dk32.at[i], dks.at[i])
        own = pl.ds(pl.multiple_of(k * 64, 64), 64)
        part = d32[i, own, :] + dk32[i]
        dk32[i] = part
        if i in NARROW:
            dpart[i] = part.astype(BF)
        for n in (2, 1, 3):
            at = pl.ds(pl.multiple_of(x_of[n] * H, H), H)
            to = (t, r, x_col[n])
            if i in NARROW:
                send(dpart.at[i, at], dr16.at[i, n - 1], "dl", drs.at[i], to)
            else:
                send(dk32.at[i, at], dr.at[i, n - 1], "d", drs.at[i], to)

    def stage_s8(i):
        came = dr16.at[i] if i in NARROW else dr.at[i]
        wait(came, drs.at[i])
        total = dk32[i, pl.ds(pl.multiple_of(x * H, H), H), :]
        for n in range(3):
            total = total + came[n].astype(F32)
        b, u = BLOCK[i], HALF[i]
        if b == 0:
            zown[u] = total
        elif i in NARROW:
            zs32[u, b] = total
            send(zs32.at[u, b], zr32.at[u, b], "zl", zrs.at[u, b], (tok_of[b], r, c))
        else:
            zs[u, b] = total.astype(BF)
            send(zs.at[u, b], zr.at[u, b], "z", zrs.at[u, b], (tok_of[b], r, c))

    def stage_s9(u):
        total = zown[u]
        for b in range(1, 4):
            narrow = any((BLOCK[i], HALF[i]) == (b, u) for i in NARROW)
            came = (zr32 if narrow else zr).at[u, b]
            wait(came, zrs.at[u, b])
            total = total + came[...].astype(F32)
        at = pl.ds(pl.multiple_of(u * T + (k * 4 + x) * H, H), H)
        obuf[at, :] = total.astype(BF)
        for n in (2, 1, 3):
            for core in range(2):
                send(obuf.at[at], obuf.at[at], "o", ors.at[u], (t, r, x_of[n] * 2 + core))
        send(obuf.at[at], obuf.at[at], "o", ors.at[u], at_core)

    tn = (((0,), (0,)), ((), ()))

    def stage_g(n):
        if n == 2:
            tall[...] = lax.dot_general(
                hid[...], tc[1], tn, preferred_element_type=F32
            )
            finish(tall, dr_w, dk, down_g, down_s)
            return
        full[...] = lax.dot_general(
            tc[0], act[:, pl.ds(512 * n, 512)], tn, preferred_element_type=F32
        )
        if n == 0:
            finish(full, gr, gk, gate_g, gate_s)
        else:
            finish(full, ur, uk, up_g, up_s)

    def prepare(n):
        loads[2 + 2 * n].wait()
        loads[3 + 2 * n].wait()
        apply_mask((gr, ur, dr_w)[n], (gk, uk, dk)[n], (gw, uw, dw)[n])
        forward(0, n)

    loads[0].wait()
    loads[1].wait()
    prepare(0)
    pl.semaphore_wait(barrier, len(peers))
    for i in range(NCH):
        if BLOCK[i] and ("az", i) not in ORDER:
            stage_az(i)
    prepare(1)
    prepare(2)
    stages = dict(
        az=stage_az, ax=stage_ax, ac=stage_ac, s1=stage_s1, s2=stage_s2, s3=stage_s3, s4=stage_s4,
        s5=stage_s5, s6=stage_s6, s7=stage_s7, s7b=stage_s7b, s8=stage_s8, t4=stage_t4,
        t5=stage_t5, t6=stage_t6, t7=stage_t7, s9=stage_s9, g=stage_g,
    )
    for name, i in ORDER:
        stages[name](i)
    for u in range(2):
        wait(obuf.at[pl.ds(0, 7 * H)], ors.at[u])
    wait(tc.at[0, pl.ds(0, 8 * 32)], send_sem.at[0])
    wait(tc.at[0, pl.ds(0, 16 * 32)], send_sem.at[1])
    wait(tc.at[0, pl.ds(0, 6 * T)], send_sem.at[2])
    whole, narrow = len(WHOLE), len(NARROW)
    wait(pre.at[pl.ds(0, (56 + whole) * H)], send_sem.at[3])
    wait(act.at[pl.ds(0, (56 - whole) * H)], send_sem.at[4])
    wait(dr.at[pl.ds(0, NCH - narrow)], send_sem.at[5])
    far = sum(1 for i in range(NCH) if BLOCK[i] and i not in NARROW)
    wait(obuf.at[pl.ds(0, far * H)], send_sem.at[6])
    wait(obuf.at[pl.ds(0, 14 * H)], send_sem.at[7])
    wait(dk32, send_sem.at[8])
    wait(dr16.at[pl.ds(0, narrow)], send_sem.at[9])
    if far < 6:
        wait(dk32.at[0, pl.ds(0, (6 - far) * H)], send_sem.at[10])
    wait(hid.at[pl.ds(0, (56 - whole) * H)], send_sem.at[11])


def store_kernel(*refs):
    n = len(refs) // 2
    sems = refs[-1]
    copies = [
        pltpu.make_async_copy(refs[i], refs[n + i], sems.at[i]) for i in range(n)
    ]
    for copy in copies:
        copy.start()
    for copy in copies:
        copy.wait()


def on_device(*args):
    hbm = pl.BlockSpec(memory_space=pltpu.HBM)
    vmem = pl.BlockSpec(memory_space=pltpu.VMEM)
    dma = pltpu.SemaphoreType.DMA
    shapes = ((256, 1024),) + ((1024, 512), (1024, 512), (512, 1024)) * 2
    args = [pltpu.with_memory_space_constraint(a, pltpu.HBM) for a in args]
    outs = pl.pallas_call(
        comm_kernel,
        name="exchange",
        out_shape=[pltpu.VMEM(s, BF) for s in shapes],
        in_specs=[hbm] * 8,
        out_specs=[vmem] * 7,
        scratch_shapes=[
            pltpu.VMEM((2, 1024, 1024), BF),
            pltpu.VMEM((1024, 512), BF),
            pltpu.VMEM((1024, 512), BF),
            pltpu.VMEM((512, 1024), BF),
            pltpu.VMEM((1024, 512), BF),
            pltpu.VMEM((1024, 512), BF),
            pltpu.VMEM((512, 1024), BF),
            pltpu.VMEM((64, 512), jnp.int32),
            pltpu.VMEM((64, 512), jnp.int32),
            pltpu.VMEM((32, 1024), jnp.int32),
            pltpu.VMEM((1024, 1536), BF),
            pltpu.VMEM((1024, 1536), F32),
            pltpu.VMEM((NCH, 2, H, 1536), BF),
            pltpu.VMEM((NCH, 2, H, 1536), BF),
            pltpu.VMEM((NCH, 4, H, 1536), BF),
            pltpu.VMEM((NCH, 2 * H, 1536), BF),
            pltpu.VMEM((NCH, 2 * H, 1536), BF),
            pltpu.VMEM((NCH, 2 * H, 1536), F32),
            pltpu.VMEM((1024, 1024), BF),
            pltpu.VMEM((1024, 512), BF),
            pltpu.VMEM((NCH, 64, 1024), BF),
            pltpu.VMEM((NCH, T, 1024), F32),
            pltpu.VMEM((NCH, 64, 1024), F32),
            pltpu.VMEM((NCH, 3, H, 1024), F32),
            pltpu.VMEM((NCH, 3, H, 1024), BF),
            pltpu.VMEM((2, H, 1024), F32),
            pltpu.VMEM((2, 4, H, 1024), BF),
            pltpu.VMEM((2, 4, H, 1024), BF),
            pltpu.VMEM((2, 4, H, 1024), F32),
            pltpu.VMEM((2, 4, H, 1024), F32),
            pltpu.VMEM((1024, 512), F32),
            pltpu.VMEM((512, 1024), F32),
            dma((8,)),
            dma((12,)),
            dma((NCH,)),
            dma((NCH,)),
            dma((NCH,)),
            dma((NCH,)),
            dma((NCH,)),
            dma((NCH,)),
            dma((NCH,)),
            dma((NCH, 2)),
            dma((NCH,)),
            dma((NCH, 2)),
            dma((NCH,)),
            dma((NCH,)),
            dma((2, 4)),
            dma((2,)),
        ],
        compiler_params=pltpu.CompilerParams(
            collective_id=0, has_side_effects=True, vmem_limit_bytes=50 * 2**20
        ),
    )(*args)
    return tuple(
        pl.pallas_call(
            store_kernel,
            name="store",
            out_shape=[jax.ShapeDtypeStruct(s, BF) for s in shapes],
            in_specs=[vmem] * 7,
            out_specs=[hbm] * 7,
            scratch_shapes=[dma((7,))],
            compiler_params=pltpu.CompilerParams(vmem_limit_bytes=2**20),
        )(*[pltpu.with_memory_space_constraint(o, pltpu.VMEM) for o in outs])
    )


def solution(mesh):
    return jax.shard_map(
        on_device,
        mesh=mesh,
        in_specs=(
            P("tok", "row"),
            P("tok", "row"),
            P("row", ("tok", "col")),
            P("row", ("tok", "col")),
            P(("tok", "col"), "row"),
            P("row", ("tok", "col")),
            P("row", ("tok", "col")),
            P(("tok", "col"), "row"),
        ),
        out_specs=(
            P("tok", "row"),
            P("row", ("tok", "col")),
            P("row", ("tok", "col")),
            P(("tok", "col"), "row"),
            P("row", ("tok", "col")),
            P("row", ("tok", "col")),
            P(("tok", "col"), "row"),
        ),
        check_vma=False,
    )
```

```python
import functools

import jax
import jax.numpy as jnp
from jax import lax
from jax.experimental import pallas as pl
from jax.experimental.pallas import tpu as pltpu
from jax.sharding import PartitionSpec as P

MESH = pl.DeviceIdType.MESH
BF = jnp.bfloat16
F32 = jnp.float32
NCH = 8
T = 128
H = 16
BLOCK = (0, 0, 1, 2, 3, 3, 2, 1)
HALF = (0, 1, 0, 0, 0, 1, 1, 1)
WHOLE = (7,)
NARROW = (0, 1, 7,)
ORDER = (
    ("s1", 0), ("s2", 0), ("az", 5), ("az", 6), ("ax", 2), ("s1", 1), ("ax", 3), ("s3", 0), ("ac", 2),
    ("ax", 4), ("s2", 1), ("s1", 2), ("ac", 3), ("ax", 5), ("az", 7), ("s1", 3), ("s3", 1), ("ac", 4),
    ("s2", 2), ("ax", 6), ("s1", 4), ("s2", 3), ("ac", 5), ("s4", 0), ("s3", 2), ("ax", 7), ("s1", 5),
    ("ac", 6), ("s2", 4), ("s3", 3), ("s1", 6), ("s2", 5), ("s5", 0), ("s4", 2), ("s3", 4), ("s2", 6),
    ("s4", 3), ("ac", 7), ("s3", 5), ("s5", 2), ("s6", 0), ("s1", 7), ("s3", 6), ("s5", 3), ("s6", 2),
    ("s4", 4), ("s7", 0), ("s2", 7), ("s4", 5), ("s6", 3), ("s7b", 0), ("s4", 6), ("s7", 2), ("s5", 4),
    ("s3", 7), ("s4", 1), ("t4", 4), ("s5", 5), ("s7b", 2), ("s7", 3), ("s8", 0), ("s6", 4), ("s5", 6),
    ("t4", 2), ("t4", 6), ("s7b", 3), ("s6", 5), ("t4", 0), ("t4", 5), ("s7", 4), ("s6", 6), ("t4", 1),
    ("s8", 2), ("s4", 7), ("s7b", 4), ("s7", 5), ("s5", 1), ("s7", 6), ("s8", 3), ("s7b", 5), ("s6", 7),
    ("t4", 3), ("s7b", 6), ("s6", 1), ("t5", 5), ("t5", 6), ("t4", 7), ("t5", 0), ("t5", 2), ("t5", 1),
    ("s7", 7), ("s8", 4), ("s7", 1), ("s8", 5), ("s7b", 7), ("t6", 0), ("t5", 4), ("t5", 3), ("s7b", 1),
    ("t6", 7), ("t6", 5), ("t6", 2), ("s8", 6), ("s9", 0), ("s8", 7), ("t6", 6), ("g", 0), ("t6", 1),
    ("t6", 4), ("t7", 6), ("s8", 1), ("t6", 3), ("s9", 1), ("t7", 7), ("g", 1), ("t7", 3), ("t7", 0),
    ("t7", 4), ("t7", 2), ("t7", 5), ("t7", 1), ("g", 2),
)


def unpack(keep_ref, i, shifts):
    row = jnp.broadcast_to(keep_ref[pl.ds(i, 1), :], shifts.shape)
    return (jnp.right_shift(row, shifts) & 1).astype(F32)


def for_row_groups(keep_ref, body):
    shifts = lax.broadcasted_iota(jnp.int32, (16, keep_ref.shape[1]), 0)

    def one(i, _):
        body(pl.ds(pl.multiple_of(i * 16, 16), 16), unpack(keep_ref, i, shifts))
        return 0

    lax.fori_loop(0, keep_ref.shape[0], one, 0, unroll=4)


def apply_mask(w_ref, keep_ref, eff_ref):
    def body(at, bits):
        eff_ref[at, :] = (w_ref[at, :].astype(F32) * bits).astype(BF)

    for_row_groups(keep_ref, body)


def finish(full_ref, w_ref, keep_ref, grad_ref, score_ref):
    def body(at, bits):
        full = full_ref[at, :]
        grad_ref[at, :] = (full * bits).astype(BF)
        score_ref[at, :] = (-(w_ref[at, :].astype(F32) * full)).astype(BF)

    for_row_groups(keep_ref, body)


def comm_kernel(
    tokens, cot, gate_w, up_w, down_w, gate_k, up_k, down_k,
    obuf, gate_g, up_g, down_g, gate_s, up_s, down_s,
    tc, gr, ur, dr_w, gw, uw, dw, gk, uk, dk, pre, pre32, rx1, acc, rx3, hs, hr, keep, act, hid,
    dpart, d32, dk32, dr, dr16, zown, zs, zr, zs32, zr32, full, tall,
    ld_sem, send_sem, az, ax, ac, s1, s3, hrs, gh, gy, th, ty, dks, drs, zrs, ors,
):
    t = lax.axis_index("tok")
    r = lax.axis_index("row")
    c = lax.axis_index("col")
    rem = lax.rem
    h, k = rem(r, 2), rem(c, 2)
    y, x = lax.div(r, 2), lax.div(c, 2)
    y_next, y_prev, y_opp = rem(y + 1, 4), rem(y + 3, 4), rem(y + 2, 4)
    x_of = [rem(x + n, 4) for n in range(4)]
    x_col = [at_x * 2 + k for at_x in x_of]
    col_of = [rem(c + n, 8) for n in range(8)]
    at_next, at_prev = (t, y_next * 2 + h, c), (t, y_prev * 2 + h, c)
    at_twin = (t, y * 2 + (1 - h), c)
    at_core = (t, r, x * 2 + (1 - k))

    t0, t1 = rem(t, 2), lax.div(t, 2)
    tok_of = [rem(t0 + n % 2, 2) + 2 * rem(t1 + n // 2, 2) for n in range(4)]
    base_of = [[pl.multiple_of(b * 256 + u * T, T) for u in range(2)] for b in tok_of]

    barrier = pltpu.get_barrier_semaphore()
    peers = [at_next, at_prev, at_twin]
    peers += [(t, r, col_of[n]) for n in range(1, 8)]
    peers += [(tok_of[n], r, c) for n in range(1, 4)]
    for peer in peers:
        pl.semaphore_signal(barrier, inc=1, device_id=peer, device_id_type=MESH)

    mine = pl.ds(pl.multiple_of(t * 256, 256), 256)
    loads = [
        pltpu.make_async_copy(src, dst, ld_sem.at[n])
        for n, (src, dst) in enumerate(
            (
                (tokens, tc.at[0, mine]), (cot, tc.at[1, mine]),
                (gate_k, gk), (gate_w, gr), (up_k, uk), (up_w, ur),
                (down_k, dk), (down_w, dr_w),
            )
        )
    ]
    for copy in loads:
        copy.start()

    SEND = dict(az=0, ax=1, ac=2, rs=3, ag=4, d=5, z=6, o=7, dk=8, dl=9, zl=10, t=11)

    def send(src, dst, cls, recv, peer):
        pltpu.make_async_remote_copy(
            src_ref=src, dst_ref=dst, send_sem=send_sem.at[SEND[cls]], recv_sem=recv,
            device_id=peer, device_id_type=MESH,
        ).start()

    def wait(ref, sem):
        pltpu.make_async_copy(ref, ref, sem).wait()

    def base(i):
        return base_of[BLOCK[i]][HALF[i]]

    def rows(i, q, n=H):
        return pl.ds(pl.multiple_of(base(i) + q * n, n), n)

    def stage_az(i):
        for n in (0, 2) if BLOCK[i] == 1 else (0,):
            start = base_of[0][HALF[i]] + x_of[n] * 32
            at = pl.ds(pl.multiple_of(start, 32), 32)
            send(tc.at[k, at], tc.at[k, at], "az", az.at[i], (tok_of[BLOCK[i]], r, c))

    def stage_ax(i):
        near = BLOCK[i] == 1
        at = rows(i, x, 32)
        wait(tc.at[k, pl.ds(0, 64 if near else 32)], az.at[i])
        for n in (1, 3) if near else (2, 1, 3):
            send(tc.at[k, at], tc.at[k, at], "ax", ax.at[i], (t, r, x_col[n]))

    def stage_ac(i):
        wait(tc.at[k, pl.ds(0, 64 if BLOCK[i] == 1 else 96)], ax.at[i])
        at = rows(i, 0, T)
        send(tc.at[k, at], tc.at[k, at], "ac", ac.at[i], at_core)

    def forward(i, n):
        at = rows(i, 0, T)
        if n == 2:
            part = lax.dot_general(
                tc[1, at, :], dw[...], (((1,), (1,)), ((), ())), preferred_element_type=F32
            )
        else:
            part = jnp.dot(tc[0, at, :], (gw, uw)[n][...], preferred_element_type=F32)
        pre32[at, pl.ds(n * 512, 512)] = part
        pre[at, pl.ds(n * 512, 512)] = part.astype(BF)

    def stage_s1(i):
        if BLOCK[i]:
            wait(tc.at[1 - k, rows(i, 0, T)], ac.at[i])
        if i:
            for n in range(3):
                forward(i, n)
        send(pre.at[rows(i, y_opp * 2)], rx1.at[i, 0], "rs", s1.at[i], at_next)
        send(pre.at[rows(i, y_opp * 2 + 1)], rx1.at[i, 1], "rs", s1.at[i], at_prev)
        send(pre.at[rows(i, y_next * 2 + 1)], rx3.at[i, 0], "rs", s3.at[i], at_next)
        send(pre.at[rows(i, y_prev * 2)], rx3.at[i, 1], "rs", s3.at[i], at_prev)

    def stage_s2(i):
        wait(rx1.at[i], s1.at[i])
        acc[i, 0] = (rx1[i, 0].astype(F32) + pre32[rows(i, y_next * 2), :]).astype(BF)
        send(acc.at[i, 0], rx3.at[i, 2], "rs", s3.at[i], at_next)
        acc[i, 1] = (rx1[i, 1].astype(F32) + pre32[rows(i, y_prev * 2 + 1), :]).astype(BF)
        send(acc.at[i, 1], rx3.at[i, 3], "rs", s3.at[i], at_prev)

    def stage_s3(i):
        wait(rx3.at[i], s3.at[i])

        def total(half):
            return (
                pre32[rows(i, y * 2 + half), :]
                + rx3[i, 1 - half].astype(F32)
                + rx3[i, 2 + half].astype(F32)
            )

        if i in WHOLE:
            for half in range(2):
                part = total(half)
                hs[i, pl.ds(half * H, H)] = part.astype(BF)
                keep[i, pl.ds(half * H, H)] = part
            send(hs.at[i], hr.at[i], "rs", hrs.at[i], at_twin)
        else:
            first = pl.ds(0, H)
            hs[i, first] = total(1 - h).astype(BF)
            send(hs.at[i, first], hr.at[i, first], "rs", hrs.at[i], at_twin)
            keep[i, first] = total(h)

    def own_rows(i):
        return rows(i, y, 2 * H) if i in WHOLE else rows(i, r)

    def stage_s4(i):
        got = pl.ds(0, 2 * H if i in WHOLE else H)
        wait(hr.at[i, got], hrs.at[i])
        sums = keep[i, got] + hr[i, got].astype(F32)
        gate, up, back = sums[:, :512], sums[:, 512:1024], sums[:, 1024:]
        sig = jax.nn.sigmoid(gate)
        silu = gate * sig
        at = own_rows(i)
        hid[at, :] = (silu * up).astype(BF)
        act[at, pl.ds(0, 512)] = (back * up * (sig * (1.0 + gate * (1.0 - sig)))).astype(BF)
        act[at, pl.ds(512, 512)] = (back * silu).astype(BF)
        gather_own(i, act, "ag", gh, gy)

    def gather_own(i, ref, cls, twin_sem, ring_sem):
        at = own_rows(i)
        if i in WHOLE:
            send(ref.at[at], ref.at[at], cls, ring_sem.at[i, 0], at_next)
            send(ref.at[at], ref.at[at], cls, ring_sem.at[i, 0], at_prev)
            return
        send(ref.at[at], ref.at[at], cls, twin_sem.at[i], at_twin)
        send(ref.at[at], ref.at[at], cls, ring_sem.at[i, h], at_next)
        send(ref.at[at], ref.at[at], cls, ring_sem.at[i, 1 - h], at_prev)

    def gather_twin(i, ref, cls, twin_sem, ring_sem):
        at = rows(i, y * 2 + (1 - h))
        wait(ref.at[at], twin_sem.at[i])
        send(ref.at[at], ref.at[at], cls, ring_sem.at[i, 1 - h], at_next)
        send(ref.at[at], ref.at[at], cls, ring_sem.at[i, h], at_prev)

    def gather_far(i, ref, cls, ring_sem):
        wait(ref.at[pl.ds(0, (4 if i in WHOLE else 2) * H)], ring_sem.at[i, 0])
        at = rows(i, y_prev * 2)
        send(ref.at[at], ref.at[at], cls, ring_sem.at[i, 1], at_next)
        at = rows(i, y_next * 2 + 1)
        send(ref.at[at], ref.at[at], cls, ring_sem.at[i, 1], at_prev)

    def stage_s5(i):
        gather_twin(i, act, "ag", gh, gy)

    def stage_s6(i):
        gather_far(i, act, "ag", gy)

    def stage_t4(i):
        gather_own(i, hid, "t", th, ty)

    def stage_t5(i):
        gather_twin(i, hid, "t", th, ty)

    def stage_t6(i):
        gather_far(i, hid, "t", ty)

    def stage_t7(i):
        wait(hid.at[pl.ds(0, (2 if i in WHOLE else 4) * H)], ty.at[i, 1])

    def stage_s7(i):
        wait(act.at[pl.ds(0, (2 if i in WHOLE else 4) * H)], gy.at[i, 1])
        at = rows(i, 0, T)
        nt = (((1,), (1,)), ((), ()))
        part = lax.dot_general(
            act[at, pl.ds(0, 512)], gw[...], nt, preferred_element_type=F32
        ) + lax.dot_general(
            act[at, pl.ds(512, 512)], uw[...], nt, preferred_element_type=F32
        )
        d32[i] = part
        other = pl.ds(pl.multiple_of((1 - k) * 64, 64), 64)
        send(d32.at[i, other], dk32.at[i], "dk", dks.at[i], at_core)

    def stage_s7b(i):
        wait(dk32.at[i], dks.at[i])
        own = pl.ds(pl.multiple_of(k * 64, 64), 64)
        part = d32[i, own, :] + dk32[i]
        dk32[i] = part
        if i in NARROW:
            dpart[i] = part.astype(BF)
        for n in (2, 1, 3):
            at = pl.ds(pl.multiple_of(x_of[n] * H, H), H)
            to = (t, r, x_col[n])
            if i in NARROW:
                send(dpart.at[i, at], dr16.at[i, n - 1], "dl", drs.at[i], to)
            else:
                send(dk32.at[i, at], dr.at[i, n - 1], "d", drs.at[i], to)

    def stage_s8(i):
        came = dr16.at[i] if i in NARROW else dr.at[i]
        wait(came, drs.at[i])
        total = dk32[i, pl.ds(pl.multiple_of(x * H, H), H), :]
        for n in range(3):
            total = total + came[n].astype(F32)
        b, u = BLOCK[i], HALF[i]
        if b == 0:
            zown[u] = total
        elif i in NARROW:
            zs32[u, b] = total
            send(zs32.at[u, b], zr32.at[u, b], "zl", zrs.at[u, b], (tok_of[b], r, c))
        else:
            zs[u, b] = total.astype(BF)
            send(zs.at[u, b], zr.at[u, b], "z", zrs.at[u, b], (tok_of[b], r, c))

    def stage_s9(u):
        total = zown[u]
        for b in range(1, 4):
            narrow = any((BLOCK[i], HALF[i]) == (b, u) for i in NARROW)
            came = (zr32 if narrow else zr).at[u, b]
            wait(came, zrs.at[u, b])
            total = total + came[...].astype(F32)
        at = pl.ds(pl.multiple_of(u * T + (k * 4 + x) * H, H), H)
        obuf[at, :] = total.astype(BF)
        for n in (2, 1, 3):
            for core in range(2):
                send(obuf.at[at], obuf.at[at], "o", ors.at[u], (t, r, x_of[n] * 2 + core))
        send(obuf.at[at], obuf.at[at], "o", ors.at[u], at_core)

    tn = (((0,), (0,)), ((), ()))

    def stage_g(n):
        if n == 2:
            tall[...] = lax.dot_general(
                hid[...], tc[1], tn, preferred_element_type=F32
            )
            finish(tall, dr_w, dk, down_g, down_s)
            return
        full[...] = lax.dot_general(
            tc[0], act[:, pl.ds(512 * n, 512)], tn, preferred_element_type=F32
        )
        if n == 0:
            finish(full, gr, gk, gate_g, gate_s)
        else:
            finish(full, ur, uk, up_g, up_s)

    def prepare(n):
        loads[2 + 2 * n].wait()
        loads[3 + 2 * n].wait()
        apply_mask((gr, ur, dr_w)[n], (gk, uk, dk)[n], (gw, uw, dw)[n])
        forward(0, n)

    loads[0].wait()
    loads[1].wait()
    prepare(0)
    prepare(1)
    pl.semaphore_wait(barrier, len(peers))
    for i in range(NCH):
        if BLOCK[i] and ("az", i) not in ORDER:
            stage_az(i)
    prepare(2)
    stages = dict(
        az=stage_az, ax=stage_ax, ac=stage_ac, s1=stage_s1, s2=stage_s2, s3=stage_s3, s4=stage_s4,
        s5=stage_s5, s6=stage_s6, s7=stage_s7, s7b=stage_s7b, s8=stage_s8, t4=stage_t4,
        t5=stage_t5, t6=stage_t6, t7=stage_t7, s9=stage_s9, g=stage_g,
    )
    for name, i in ORDER:
        stages[name](i)
    for u in range(2):
        wait(obuf.at[pl.ds(0, 7 * H)], ors.at[u])
    wait(tc.at[0, pl.ds(0, 8 * 32)], send_sem.at[0])
    wait(tc.at[0, pl.ds(0, 16 * 32)], send_sem.at[1])
    wait(tc.at[0, pl.ds(0, 6 * T)], send_sem.at[2])
    whole, narrow = len(WHOLE), len(NARROW)
    wait(pre.at[pl.ds(0, (56 + whole) * H)], send_sem.at[3])
    wait(act.at[pl.ds(0, (56 - whole) * H)], send_sem.at[4])
    wait(dr.at[pl.ds(0, NCH - narrow)], send_sem.at[5])
    far = sum(1 for i in range(NCH) if BLOCK[i] and i not in NARROW)
    wait(obuf.at[pl.ds(0, far * H)], send_sem.at[6])
    wait(obuf.at[pl.ds(0, 14 * H)], send_sem.at[7])
    wait(dk32, send_sem.at[8])
    wait(dr16.at[pl.ds(0, narrow)], send_sem.at[9])
    if far < 6:
        wait(dk32.at[0, pl.ds(0, (6 - far) * H)], send_sem.at[10])
    wait(hid.at[pl.ds(0, (56 - whole) * H)], send_sem.at[11])


def store_kernel(*refs):
    n = len(refs) // 2
    sems = refs[-1]
    copies = [
        pltpu.make_async_copy(refs[i], refs[n + i], sems.at[i]) for i in range(n)
    ]
    for copy in copies:
        copy.start()
    for copy in copies:
        copy.wait()


def on_device(*args):
    hbm = pl.BlockSpec(memory_space=pltpu.HBM)
    vmem = pl.BlockSpec(memory_space=pltpu.VMEM)
    dma = pltpu.SemaphoreType.DMA
    shapes = ((256, 1024),) + ((1024, 512), (1024, 512), (512, 1024)) * 2
    args = [pltpu.with_memory_space_constraint(a, pltpu.HBM) for a in args]
    outs = pl.pallas_call(
        comm_kernel,
        name="exchange",
        out_shape=[pltpu.VMEM(s, BF) for s in shapes],
        in_specs=[hbm] * 8,
        out_specs=[vmem] * 7,
        scratch_shapes=[
            pltpu.VMEM((2, 1024, 1024), BF),
            pltpu.VMEM((1024, 512), BF),
            pltpu.VMEM((1024, 512), BF),
            pltpu.VMEM((512, 1024), BF),
            pltpu.VMEM((1024, 512), BF),
            pltpu.VMEM((1024, 512), BF),
            pltpu.VMEM((512, 1024), BF),
            pltpu.VMEM((64, 512), jnp.int32),
            pltpu.VMEM((64, 512), jnp.int32),
            pltpu.VMEM((32, 1024), jnp.int32),
            pltpu.VMEM((1024, 1536), BF),
            pltpu.VMEM((1024, 1536), F32),
            pltpu.VMEM((NCH, 2, H, 1536), BF),
            pltpu.VMEM((NCH, 2, H, 1536), BF),
            pltpu.VMEM((NCH, 4, H, 1536), BF),
            pltpu.VMEM((NCH, 2 * H, 1536), BF),
            pltpu.VMEM((NCH, 2 * H, 1536), BF),
            pltpu.VMEM((NCH, 2 * H, 1536), F32),
            pltpu.VMEM((1024, 1024), BF),
            pltpu.VMEM((1024, 512), BF),
            pltpu.VMEM((NCH, 64, 1024), BF),
            pltpu.VMEM((NCH, T, 1024), F32),
            pltpu.VMEM((NCH, 64, 1024), F32),
            pltpu.VMEM((NCH, 3, H, 1024), F32),
            pltpu.VMEM((NCH, 3, H, 1024), BF),
            pltpu.VMEM((2, H, 1024), F32),
            pltpu.VMEM((2, 4, H, 1024), BF),
            pltpu.VMEM((2, 4, H, 1024), BF),
            pltpu.VMEM((2, 4, H, 1024), F32),
            pltpu.VMEM((2, 4, H, 1024), F32),
            pltpu.VMEM((1024, 512), F32),
            pltpu.VMEM((512, 1024), F32),
            dma((8,)),
            dma((12,)),
            dma((NCH,)),
            dma((NCH,)),
            dma((NCH,)),
            dma((NCH,)),
            dma((NCH,)),
            dma((NCH,)),
            dma((NCH,)),
            dma((NCH, 2)),
            dma((NCH,)),
            dma((NCH, 2)),
            dma((NCH,)),
            dma((NCH,)),
            dma((2, 4)),
            dma((2,)),
        ],
        compiler_params=pltpu.CompilerParams(
            collective_id=0, has_side_effects=True, vmem_limit_bytes=50 * 2**20
        ),
    )(*args)
    return tuple(
        pl.pallas_call(
            store_kernel,
            name="store",
            out_shape=[jax.ShapeDtypeStruct(s, BF) for s in shapes],
            in_specs=[vmem] * 7,
            out_specs=[hbm] * 7,
            scratch_shapes=[dma((7,))],
            compiler_params=pltpu.CompilerParams(vmem_limit_bytes=2**20),
        )(*[pltpu.with_memory_space_constraint(o, pltpu.VMEM) for o in outs])
    )


def solution(mesh):
    return jax.shard_map(
        on_device,
        mesh=mesh,
        in_specs=(
            P("tok", "row"),
            P("tok", "row"),
            P("row", ("tok", "col")),
            P("row", ("tok", "col")),
            P(("tok", "col"), "row"),
            P("row", ("tok", "col")),
            P("row", ("tok", "col")),
            P(("tok", "col"), "row"),
        ),
        out_specs=(
            P("tok", "row"),
            P("row", ("tok", "col")),
            P("row", ("tok", "col")),
            P(("tok", "col"), "row"),
            P("row", ("tok", "col")),
            P("row", ("tok", "col")),
            P(("tok", "col"), "row"),
        ),
        check_vma=False,
    )
```
